32 devices in a mesh: groups: 2 (over x), serve: 16 (over z, y, core), tensor: 1.
Axes of the slice: x: 2, y: 2, z: 4, core: 2. Of those that a mesh axis runs over, the one named last changes fastest.
Arguments:
- span_states: bfloat16 [32, 256, 12288], P(('groups', 'serve'), None, 'tensor'), parts along dimension 0, may hold values from -6 to 6
- recomp_states: bfloat16 [32, 240, 12288], P(('groups', 'serve'), None, 'tensor'), parts along dimension 0, may hold values from -24 to 24
- w_query: bfloat16 [12288, 6, 128], P('tensor', None, 'serve'), may hold values from -0.054126588 to 0.054126588
- w_kv: bfloat16 [12288, 2, 128], P('tensor', None, 'serve'), may hold values from -0.054126588 to 0.054126588
- w_out: bfloat16 [6, 128, 1, 12288], P('tensor', None, None, 'serve'), may hold values from -0.21875 to 0.21875
- span_map: int32 [32, 6], P(('groups', 'serve')), parts along dimension 0, may hold values from 0 to 15, all different within a row
- span_lengths: int32 [32], P(('groups', 'serve')), parts along dimension 0, may hold values from 128 to 256, as said below
- recompute_idx: int32 [32, 240], P(('groups', 'serve')), parts along dimension 0, may hold values from 0 to 1407, as said below
- block_table: int32 [512], P(('groups', 'serve')), parts along dimension 0, may hold values from 0 to 15, as said below
Outputs:
- kv_cache: bfloat16 [512, 16, 256], P(('groups', 'serve')), parts along dimension 0
- attn_out: bfloat16 [32, 240, 12288], P(('groups', 'serve'), None, 'tensor'), parts along dimension 0
The draws below stay inside these ranges and needn't reach their ends.
There are 2 independent parts, one for each index of `groups`. The reference program is written for one: setup_inputs(seed, part) draws one part's arguments, and reference() takes and returns one part's arrays. A program takes and returns all parts, laid end to end along the dimension named above; an argument that names none is the same for every part. Nothing has to cross between parts.
Inputs may be any that keep to these rules, and one draw needn't show every extreme that they name: `span_lengths`: some span has exactly 256 live tokens and some exactly 128. `recompute_idx`: entries s * 40 to (s + 1) * 40 - 1 of a row are distinct positions s * 256 + o with o < 128. `block_table`: each span's 16 entries are a permutation of 0 to 15. `span_map`: A row names 6 different spans; every span is named by some row.
All inputs are finite; a program needn't handle non-finite values.
Results may differ from the reference program's by a relative error of at most 0.014.
Values may be sent and summed in bfloat16 or wider, within the bound.
No kernel may reach another device: no remote copies, remote signals or barrier semaphores. Data moves between devices by JAX's collectives and lax.ppermute only.
A program may use at most 128 MiB of HBM per device.

```python
import jax
import jax.numpy as jnp
from jax import lax

D = 12288
HD = 128
QH = 6
SPAN = 256
PAGE = 16
CPR = 6
NCH = 16
REQS = 16
PPC = 16
RSLOT = 40
RECOMP = 240
HPC = 6
DCORE = 12288
N_TENSOR = 1


def shared_kv_columns(key):
    own_key = jax.random.fold_in(key, 101)
    values = jax.random.normal(own_key, (D, 2, HD), jnp.float32)
    return jnp.clip(values, -6.0, 6.0) * D ** (-0.5)


def draw_w_kv(key, part):
    return shared_kv_columns(key).astype(jnp.bfloat16)


def draw_w_query(key, part):
    key = jax.random.fold_in(key, 21)
    base = jnp.clip(jax.random.normal(key, (D, QH, HD), jnp.float32), -6.0, 6.0) * D ** (-0.5)
    return base.astype(jnp.bfloat16)


def draw_recomp_states(key, part):
    key = jax.random.fold_in(key, 14)
    key_base = jax.random.fold_in(key, 0)
    return jnp.clip(jax.random.normal(key_base, (REQS, RECOMP, D), jnp.float32), -6.0, 6.0).astype(jnp.bfloat16)


def draw_span_lengths(key, part):
    key = jax.random.fold_in(key, 11)
    key_lens, key_pick = jax.random.split(key)
    span_lens = jax.random.randint(key_lens, (NCH,), SPAN // 2, SPAN + 1, dtype=jnp.int32)
    picked = jax.random.randint(key_pick, (), 0, NCH, dtype=jnp.int32)
    span_lens = span_lens.at[picked].set(SPAN)
    span_lens = span_lens.at[(picked + 1) % NCH].set(SPAN // 2)
    return span_lens


def draw_recompute_idx(key, part):
    key = jax.random.fold_in(key, 12)
    row_keys = jax.random.split(key, REQS * CPR)
    offsets = jax.vmap(lambda single: jax.random.permutation(single, SPAN // 2)[:RSLOT])(row_keys)
    offsets = offsets.reshape(REQS, CPR, RSLOT).astype(jnp.int32)
    slot_base = (jnp.arange(CPR, dtype=jnp.int32) * SPAN)[None, :, None]
    return (offsets + slot_base).reshape(REQS, CPR * RSLOT)


def draw_block_table(key, part):
    key = jax.random.fold_in(key, 13)
    span_keys = jax.random.split(key, NCH)
    tables = jax.vmap(lambda single: jax.random.permutation(single, PPC))(span_keys)
    return tables.astype(jnp.int32).reshape(NCH * PPC)


def block_scale(rng, shape, shards, least, top_value):
    def one(position, parts):
        steps = jax.random.uniform(jax.random.fold_in(jax.random.fold_in(rng, 6), position), (parts,), jnp.float32, least / len(shards), top_value / len(shards))
        return jnp.repeat(jnp.exp(steps), shape[position] // parts).reshape((-1,) + (1,) * (len(shape) - position - 1))

    factor_of = one(*shards[0])
    for cut in shards[1:]:
        factor_of = factor_of * one(*cut)
    return factor_of


def distinct(stream_key, rows, count, top, lift):
    order = jax.random.permutation(jax.random.fold_in(stream_key, 1), count)
    boost = order
    for power in range(3):
        boost = boost * boost // count
    boost = boost * lift // count
    tickets = jax.random.randint(jax.random.fold_in(stream_key, 2), (rows, count), 0, 4096) + boost
    holders = jax.random.permutation(jax.random.fold_in(stream_key, 3), rows)[jnp.arange(count) % rows]
    tickets = jnp.where(jnp.arange(rows)[:, None] == holders[None, :], 1 << 14, tickets)
    score = tickets * count + jnp.arange(count)
    return lax.top_k(score.astype(jnp.int32), top)[1].astype(jnp.int32)


def gaussian(stream_key, dims, deviation, most, cuts=(), held_as=jnp.bfloat16):
    result = jax.random.normal(stream_key, dims, jnp.float32) * deviation
    if len(cuts) > 0:
        result = block_scale(stream_key, dims, cuts, -0.22, 0.18) * result
    return jnp.clip(result, min=-most, max=most).astype(held_as)


def setup_inputs(seed: int = 0, part: int = 0) -> dict:
    key_list = jax.random.split(jax.random.key(seed), 10)
    own_keys = jax.random.split(jax.random.fold_in(key_list[9], part), 10)
    span_states = gaussian(own_keys[0], (NCH, SPAN, D), 1.0, 6.0, ((0, 16),))
    recomp_states = draw_recomp_states(jax.random.fold_in(jax.random.fold_in(key_list[9], part), 71), part)
    w_query = draw_w_query(jax.random.fold_in(key_list[9], 71), part)
    w_kv = draw_w_kv(jax.random.fold_in(key_list[9], 71), part)
    w_out = gaussian(key_list[4], (QH, HD, N_TENSOR, DCORE), (QH * HD) ** -0.5, 0.21875, ((3, 16),))
    span_map = distinct(own_keys[5], REQS, NCH, CPR, 6144)
    span_lengths = draw_span_lengths(jax.random.fold_in(jax.random.fold_in(key_list[9], part), 71), part)
    recompute_idx = draw_recompute_idx(jax.random.fold_in(jax.random.fold_in(key_list[9], part), 71), part)
    block_table = draw_block_table(jax.random.fold_in(jax.random.fold_in(key_list[9], part), 71), part)
    return {"span_states": span_states, "recomp_states": recomp_states, "w_query": w_query, "w_kv": w_kv, "w_out": w_out, "span_map": span_map, "span_lengths": span_lengths, "recompute_idx": recompute_idx, "block_table": block_table}


def reference(span_states, recomp_states, w_query, w_kv, w_out, span_map, span_lengths, recompute_idx, block_table):
    kv_flat = jnp.dot(span_states.reshape(NCH * SPAN, D), w_kv.reshape(D, 2 * HD), preferred_element_type=jnp.float32).astype(jnp.bfloat16)
    logical = kv_flat.reshape(NCH, PPC, PAGE, 2 * HD)
    inverse = jnp.argsort(block_table.reshape(NCH, PPC), axis=1).astype(jnp.int32)
    kv_cache = jnp.take_along_axis(logical, inverse[:, :, None, None], axis=1).reshape(NCH * PPC, PAGE, 2 * HD)
    flat_rows = recomp_states.reshape(REQS * RECOMP, D)
    query_all = jnp.dot(flat_rows, w_query.reshape(D, QH * HD), preferred_element_type=jnp.float32).astype(jnp.bfloat16).reshape(REQS, RECOMP, QH, HD)
    new_kv = jnp.dot(flat_rows, w_kv.reshape(D, 2 * HD), preferred_element_type=jnp.float32).astype(jnp.bfloat16).reshape(REQS, RECOMP, 2, HD)
    span_kv = kv_flat.reshape(NCH, SPAN, 2, HD)

    def one_request(inputs):
        query_rows, new_rows, span_ids, positions = inputs
        gathered = span_kv[span_ids].reshape(CPR * SPAN, 2, HD)
        key_pos = jnp.arange(CPR * SPAN, dtype=jnp.int32)
        lens_here = span_lengths[span_ids]
        within = (key_pos % SPAN) < jnp.repeat(lens_here, SPAN, total_repeat_length=CPR * SPAN)
        redone = jnp.any(key_pos[:, None] == positions[None, :], axis=1)
        key_all = jnp.concatenate([gathered, new_rows], axis=0)
        pos_all = jnp.concatenate([key_pos, positions.astype(jnp.int32)])
        usable = jnp.concatenate([within & jnp.logical_not(redone), jnp.ones((RECOMP,), dtype=bool)])
        allowed = usable[None, :] & (pos_all[None, :] <= positions[:, None])
        scores = jnp.einsum('rhc,kc->rhk', query_rows.astype(jnp.float32), key_all[:, 0].astype(jnp.float32)) * (HD ** -0.5)
        scores = jnp.where(allowed[:, None, :], scores, -jnp.inf)
        weights = jax.nn.softmax(scores, axis=-1)
        return jnp.einsum('rhk,kc->rhc', weights, key_all[:, 1].astype(jnp.float32)).astype(jnp.bfloat16)

    attended = lax.map(one_request, (query_all, new_kv, span_map, recompute_idx))
    out_matrix = w_out.reshape(QH, HD, D)
    total = jnp.zeros((REQS * RECOMP, D), jnp.float32)
    for group_num in range(N_TENSOR):
        lower = group_num * HPC
        summed_heads = jnp.dot(attended[:, :, lower:lower + HPC].reshape(REQS * RECOMP, HPC * HD), out_matrix[lower:lower + HPC].reshape(HPC * HD, D), preferred_element_type=jnp.float32)
        head_part = lax.optimization_barrier(summed_heads.astype(jnp.bfloat16))
        total = total + head_part.astype(jnp.float32)
    return kv_cache, total.astype(jnp.bfloat16).reshape(REQS, RECOMP, D)
```

```python
from functools import partial
import math

import jax
import jax.numpy as jnp
import numpy as np
from jax import lax
from jax.experimental import pallas as pl
from jax.experimental.pallas import tpu as pltpu
from jax.sharding import PartitionSpec as P

HD = 128
SPAN = 256
PAGE = 16
CPR = 6
PPC = 16


def merge_block(state, query, key_rows, value_rows, allowed, score_scale):
    old_max, old_sum, old_acc = state
    scores = (
        jnp.einsum("rhc,kc->rhk", query, key_rows, preferred_element_type=jnp.float32) * score_scale
    )
    block_max = jnp.max(jnp.where(allowed, scores, -jnp.inf), axis=2)
    new_max = jnp.maximum(old_max, block_max)
    weights_now = jnp.where(allowed, jnp.exp(scores - new_max[:, :, None]), 0.0)
    rescale = jnp.exp(old_max - new_max)
    new_acc = old_acc * rescale[:, :, None] + jnp.einsum(
        "rhk,kc->rhc", weights_now, value_rows.astype(jnp.float32)
    )
    return (new_max, old_sum * rescale + jnp.sum(weights_now, axis=2), new_acc)


def general_body(
    span_states,
    recomp_states,
    w_query,
    w_kv,
    w_out,
    span_map,
    span_lengths,
    recompute_idx,
    block_table,
):
    span_rows = span_states[0]
    req_rows = recomp_states[0]
    num_recomp = req_rows.shape[0]
    all_heads = w_query.shape[1]
    query_piece = lax.all_gather(w_query, "serve", axis=2, tiled=True)
    kv_piece = lax.all_gather(w_kv, "serve", axis=2, tiled=True)
    query_part = jnp.einsum(
        "rd,dhc->rhc", req_rows, query_piece, preferred_element_type=jnp.float32
    )
    new_part = jnp.einsum("rd,dhc->rhc", req_rows, kv_piece, preferred_element_type=jnp.float32)
    span_part = jnp.einsum("rd,dhc->rhc", span_rows, kv_piece, preferred_element_type=jnp.float32)
    query_full, new_full, span_full = lax.psum((query_part, new_part, span_part), "tensor")
    core_heads = all_heads // lax.axis_size("tensor")
    my_core = lax.axis_index("tensor")
    query = lax.dynamic_slice_in_dim(query_full, my_core * core_heads, core_heads, 1).astype(
        jnp.bfloat16
    )
    new_kv = new_full.astype(jnp.bfloat16)
    span_kv = span_full.astype(jnp.bfloat16)
    logical_pages = span_kv.reshape(PPC, PAGE, 2 * HD)
    inverse = jnp.argsort(block_table)
    physical = logical_pages[inverse]
    page_lens = jnp.repeat(span_lengths, PPC, total_repeat_length=PPC)
    positions = recompute_idx[0]
    my_spans = span_map[0]
    score_scale = HD ** (-0.5)
    slot_ids = jnp.arange(CPR, dtype=jnp.int32)
    token_ids = jnp.arange(PAGE, dtype=jnp.int32)
    local_allowed = (positions[None, :] <= positions[:, None])[:, None, :]
    empty_state = (
        jnp.full((num_recomp, core_heads), -jnp.inf, jnp.float32),
        jnp.zeros((num_recomp, core_heads), jnp.float32),
        jnp.zeros((num_recomp, core_heads, HD), jnp.float32),
    )
    state = merge_block(empty_state, query, new_kv[:, 0], new_kv[:, 1], local_allowed, score_scale)

    def block_update(skipping, totals, block):
        page_data, logical, lens_block, first_page = block
        width = page_data.shape[0]
        global_page = first_page + jnp.arange(width, dtype=jnp.int32)
        span_id = global_page // PPC
        matches = my_spans[None, :] == span_id[:, None]
        in_request = jnp.any(matches, axis=1)
        slot_num = jnp.sum(jnp.where(matches, slot_ids[None, :], 0), axis=1)
        offset = logical[:, None] * PAGE + token_ids[None, :]
        key_pos = (slot_num[:, None] * SPAN + offset).reshape(width * PAGE)
        usable = (in_request[:, None] & (offset < lens_block[:, None])).reshape(width * PAGE)
        redone = jnp.any(key_pos[:, None] == positions[None, :], axis=1)
        usable = usable & jnp.logical_not(redone)
        allowed = (usable[None, :] & (key_pos[None, :] <= positions[:, None]))[:, None, :]
        key_rows = page_data.reshape(width * PAGE, 2, HD)
        result = merge_block(totals, query, key_rows[:, 0], key_rows[:, 1], allowed, score_scale)
        return (result, None)

    page_data = lax.all_gather(physical, "serve", axis=0, tiled=True)
    logical = lax.all_gather(inverse, "serve", axis=0, tiled=True)
    lens_piece = lax.all_gather(page_lens, "serve", axis=0, tiled=True)
    count = page_data.shape[0]
    block = math.gcd(count, 64)
    steps_here = count // block
    blocks = (
        page_data.reshape(steps_here, block, PAGE, 2 * HD),
        logical.reshape(steps_here, block),
        lens_piece.reshape(steps_here, block),
        jnp.arange(steps_here, dtype=jnp.int32) * block,
    )
    result, unused_out = lax.scan(partial(block_update, False), state, blocks)
    state = result
    run_max, run_sum, run_acc = state
    attended = (run_acc / run_sum[:, :, None]).astype(jnp.bfloat16)
    partial_out = jnp.einsum(
        "rhc,hctd->rtd",
        attended,
        lax.all_gather(w_out, "serve", axis=3, tiled=True),
        preferred_element_type=jnp.float32,
    )
    reduced = lax.psum_scatter(
        partial_out.astype(jnp.bfloat16), "tensor", scatter_dimension=1, tiled=True
    )
    attn_out = reduced.reshape(1, reduced.shape[0], reduced.shape[2])
    return (physical, attn_out)


CHIPS = 8
CORES = 2
RING = ((0, 0), (1, 0), (2, 0), (3, 0), (3, 1), (2, 1), (1, 1), (0, 1))
CHIP_AT = tuple((z * 2 + y) * CORES for z, y in RING)
NT = (((1,), (1,)), ((), ()))


def ring_fits(mesh):
    return tuple(mesh.shape[name] for name in ("groups", "serve", "tensor")) == (2, CHIPS * CORES, 1)


def ring_pairs(step):
    return [
        (CHIP_AT[i] + c, CHIP_AT[(i + step) % CHIPS] + c) for i in range(CHIPS) for c in range(CORES)
    ]


AHEAD, BACK = ring_pairs(1), ring_pairs(-1)
SIBLING = [(i, i ^ 1) for i in range(CHIPS * CORES)]
ACROSS = [(0, 1), (1, 0)]


def slot_table():
    table = np.zeros((CHIPS * CORES, CHIPS * CORES), np.int32)
    for i in range(CHIPS):
        for c in range(CORES):
            for slot, step in enumerate((0, -1, 1, -2, 2, -3, 3, 4)):
                chip = CHIP_AT[(i + step) % CHIPS]
                table[CHIP_AT[i] + c, slot] = chip + c
                table[CHIP_AT[i] + c, CHIPS + slot] = chip + 1 - c
    return table


def move(block, pairs):
    return lax.ppermute(block, "serve", pairs)


def across(block):
    return lax.ppermute(block, "groups", ACROSS)


def column_order(order_ref, slots, planes):
    rows, width = planes * 8, planes * HD
    row = lax.broadcasted_iota(jnp.int32, (rows, width), 0)
    col = lax.broadcasted_iota(jnp.int32, (rows, width), 1)
    place = (row // 8) * HD + row % 8
    parts = [(col == place + order_ref[p] * 8).astype(jnp.float32) for p in range(slots)]
    return jnp.concatenate(parts, axis=0).astype(jnp.bfloat16)


def kv_kernel(order_ref, table_ref, len_ref, span_ref, req_ref, *refs):
    slots = CHIPS * CORES
    w_refs = refs[:slots]
    pay_ref, new_ref, cache_ref, span_acc, req_acc = refs[slots:]
    step = pl.program_id(0)
    w = jnp.concatenate([ref[...] for ref in w_refs], axis=0)
    span_now = lax.dot_general(span_ref[0], w, NT, preferred_element_type=jnp.float32)
    req_now = lax.dot_general(req_ref[0], w, NT, preferred_element_type=jnp.float32)

    @pl.when(step == 0)
    def _():
        span_acc[...] = span_now
        req_acc[...] = req_now

    @pl.when(step > 0)
    def _():
        span_acc[...] += span_now
        req_acc[...] += req_now

    @pl.when(step == pl.num_programs(0) - 1)
    def _():
        order = column_order(order_ref, slots, 2)
        span_kv = jnp.dot(
            span_acc[...].astype(jnp.bfloat16), order, preferred_element_type=jnp.float32
        ).astype(jnp.bfloat16)
        new_ref[...] = jnp.dot(
            req_acc[...].astype(jnp.bfloat16), order, preferred_element_type=jnp.float32
        ).astype(jnp.bfloat16)
        tokens = span_kv.shape[0]
        pay_ref[0:tokens] = span_kv
        length = jnp.full((PAGE, 2 * HD), len_ref[0], jnp.int32)
        pay_ref[tokens:] = length.astype(jnp.float32).astype(jnp.bfloat16)
        for p in range(tokens // PAGE):
            cache_ref[table_ref[p]] = span_kv[p * PAGE : (p + 1) * PAGE]


def project_kv(order, block_table, span_lengths, span_states, recomp_states, w_blocks, last_block):
    tokens, width = span_states.shape[1:]
    rows = recomp_states.shape[1]
    chunk = width // 4
    per_half = width // 2 // chunk
    rows_at = w_blocks[0].shape[0] // 16 - 2

    def piece(first):
        return pl.BlockSpec((16, chunk), lambda k, *_: (first + k // per_half, k % per_half))

    half_slots = [piece(rows_at)] * (CHIPS - 1) + [piece(0)]
    blocks = w_blocks[: CHIPS - 1] + last_block[:1] + w_blocks[CHIPS - 1 :] + last_block[1:]
    return pl.pallas_call(
        kv_kernel,
        grid_spec=pltpu.PrefetchScalarGridSpec(
            num_scalar_prefetch=3,
            grid=(width // chunk,),
            in_specs=[
                pl.BlockSpec((1, tokens, chunk), lambda k, *_: (0, 0, k)),
                pl.BlockSpec((1, rows, chunk), lambda k, *_: (0, 0, k)),
                *half_slots,
                *half_slots,
            ],
            out_specs=[
                pl.BlockSpec((tokens + PAGE, 2 * HD), lambda k, *_: (0, 0)),
                pl.BlockSpec((rows, 2 * HD), lambda k, *_: (0, 0)),
                pl.BlockSpec((tokens // PAGE, PAGE, 2 * HD), lambda k, *_: (0, 0, 0)),
            ],
            scratch_shapes=[
                pltpu.VMEM((tokens, 2 * HD), jnp.float32),
                pltpu.VMEM((rows, 2 * HD), jnp.float32),
            ],
        ),
        out_shape=[
            jax.ShapeDtypeStruct((tokens + PAGE, 2 * HD), jnp.bfloat16),
            jax.ShapeDtypeStruct((rows, 2 * HD), jnp.bfloat16),
            jax.ShapeDtypeStruct((tokens // PAGE, PAGE, 2 * HD), jnp.bfloat16),
        ],
        cost_estimate=pl.CostEstimate(
            flops=2 * (tokens + rows) * width * 2 * HD,
            bytes_accessed=2 * (tokens + rows + 2 * HD) * width,
            transcendentals=0,
        ),
        compiler_params=pltpu.CompilerParams(vmem_limit_bytes=40 * 2**20),
        name="project_kv",
    )(order, block_table, span_lengths, span_states, recomp_states, *blocks)


def query_kernel(half_ref, mine_ref, other_ref, *refs):
    slots = CHIPS * CORES
    w_refs = refs[:slots]
    mine_out, other_out, mine_acc, other_acc = refs[slots:]
    step = pl.program_id(0)
    w = jnp.concatenate([ref[...] for ref in w_refs], axis=0)
    mine_now = lax.dot_general(mine_ref[0], w, NT, preferred_element_type=jnp.float32)
    other_now = lax.dot_general(other_ref[...], w, NT, preferred_element_type=jnp.float32)

    @pl.when(step == 0)
    def _():
        mine_acc[...] = mine_now
        other_acc[...] = other_now

    @pl.when(step > 0)
    def _():
        mine_acc[...] += mine_now
        other_acc[...] += other_now

    @pl.when(step == pl.num_programs(0) - 1)
    def _():
        mine_out[...] = mine_acc[...]
        other_out[...] = other_acc[...].astype(other_out.dtype)


def project_query(half, recomp_states, other_rows, w_blocks, last_block, columns):
    rows, depth = other_rows.shape
    chunk = depth // 6
    steps = depth // chunk
    part = columns // (CHIPS * CORES)
    blocks = w_blocks[: CHIPS - 1] + last_block[:1] + w_blocks[CHIPS - 1 :] + last_block[1:]
    return pl.pallas_call(
        query_kernel,
        grid_spec=pltpu.PrefetchScalarGridSpec(
            num_scalar_prefetch=1,
            grid=(steps,),
            in_specs=[
                pl.BlockSpec((1, rows, chunk), lambda k, half_ref: (0, 0, half_ref[0] * steps + k)),
                pl.BlockSpec((rows, chunk), lambda k, *_: (0, k)),
                *([pl.BlockSpec((part, chunk), lambda k, *_: (0, k))] * (CHIPS * CORES)),
            ],
            out_specs=[
                pl.BlockSpec((rows, columns), lambda k, *_: (0, 0)),
                pl.BlockSpec((rows, columns), lambda k, *_: (0, 0)),
            ],
            scratch_shapes=[
                pltpu.VMEM((rows, columns), jnp.float32),
                pltpu.VMEM((rows, columns), jnp.float32),
            ],
        ),
        out_shape=[
            jax.ShapeDtypeStruct((rows, columns), jnp.float32),
            jax.ShapeDtypeStruct((rows, columns), jnp.bfloat16),
        ],
        cost_estimate=pl.CostEstimate(
            flops=4 * rows * depth * columns,
            bytes_accessed=2 * (2 * rows + columns) * depth,
            transcendentals=0,
        ),
        compiler_params=pltpu.CompilerParams(vmem_limit_bytes=40 * 2**20),
        name="project_query",
    )(half, recomp_states, other_rows, *blocks)


def attend_kernel(map_ref, order_ref, mine_ref, other_ref, new_ref, col_ref, row_ref, *refs):
    span_refs = refs[:CPR]
    out_ref, keys, values, bias = refs[CPR:]
    rows = new_ref.shape[0]
    cached = CPR * SPAN
    padded = keys.shape[0]
    for s in range(CPR):
        keys[s * SPAN : (s + 1) * SPAN] = span_refs[s][0, 0:SPAN, 0:HD]
        values[s * SPAN : (s + 1) * SPAN] = span_refs[s][0, 0:SPAN, HD : 2 * HD]
    keys[cached : cached + rows] = new_ref[:, 0:HD]
    values[cached : cached + rows] = new_ref[:, HD : 2 * HD]
    keys[cached + rows :] = jnp.zeros((padded - cached - rows, HD), jnp.bfloat16)
    values[cached + rows :] = jnp.zeros((padded - cached - rows, HD), jnp.bfloat16)
    mine_at = jnp.broadcast_to(col_ref[...], (rows, SPAN))
    lane = lax.broadcasted_iota(jnp.int32, (rows, SPAN), 1)
    blocked = jnp.float32(-jnp.inf)
    for s in range(CPR):
        key_pos = lane + s * SPAN
        redone = jnp.max(jnp.where(mine_at == key_pos, 1.0, 0.0), axis=0, keepdims=True)
        length = span_refs[s][0, SPAN : SPAN + PAGE, :].astype(jnp.float32)[0:1]
        offset = lax.broadcasted_iota(jnp.int32, (1, SPAN), 1).astype(jnp.float32)
        usable = jnp.where(offset < length, 1.0 - redone, 0.0)
        allowed = (jnp.broadcast_to(usable, (rows, SPAN)) > 0.5) & (key_pos <= mine_at)
        bias[:, s * SPAN : (s + 1) * SPAN] = jnp.where(allowed, 0.0, blocked)
    key_pos = jnp.broadcast_to(row_ref[...], (rows, padded - cached))
    bias[:, cached:] = jnp.where(key_pos <= mine_at, 0.0, blocked)

    query = (mine_ref[...] + other_ref[...].astype(jnp.float32)).astype(jnp.bfloat16)
    heads = query.shape[1] // HD
    order = column_order(order_ref, CHIPS * CORES, heads)
    query = jnp.dot(query, order, preferred_element_type=jnp.float32).astype(jnp.bfloat16)
    for h in range(heads):
        scores = lax.dot_general(
            query[:, h * HD : (h + 1) * HD], keys[...], NT, preferred_element_type=jnp.float32
        )
        scores = scores * (HD ** (-0.5)) + bias[...]
        top = jnp.max(scores, axis=1, keepdims=True)
        weights = jnp.exp(scores - top)
        total = jnp.sum(weights, axis=1, keepdims=True)
        mixed = jnp.dot(weights.astype(jnp.bfloat16), values[...], preferred_element_type=jnp.float32)
        out_ref[:, h * HD : (h + 1) * HD] = (mixed / total).astype(jnp.bfloat16)


def attend(span_map, order, mine, other, new_kv, positions, payload):
    rows, columns = mine.shape
    cached = CPR * SPAN
    padded = cached + SPAN
    row_pos = jnp.pad(positions, (0, SPAN - rows), constant_values=2 * cached)[None, :]
    whole = lambda *shape: pl.BlockSpec(shape, lambda i, *_: (0,) * len(shape))
    slot = lambda s: pl.BlockSpec((1,) + payload.shape[1:], lambda i, map_ref, *_: (map_ref[s], 0, 0))
    return pl.pallas_call(
        attend_kernel,
        grid_spec=pltpu.PrefetchScalarGridSpec(
            num_scalar_prefetch=2,
            grid=(1,),
            in_specs=[
                whole(rows, columns),
                whole(rows, columns),
                whole(rows, 2 * HD),
                whole(rows, 1),
                whole(1, SPAN),
                *[slot(s) for s in range(CPR)],
            ],
            out_specs=whole(rows, columns),
            scratch_shapes=[
                pltpu.VMEM((padded, HD), jnp.bfloat16),
                pltpu.VMEM((padded, HD), jnp.bfloat16),
                pltpu.VMEM((rows, padded), jnp.float32),
            ],
        ),
        out_shape=jax.ShapeDtypeStruct((rows, columns), jnp.bfloat16),
        cost_estimate=pl.CostEstimate(
            flops=4 * rows * columns * padded,
            bytes_accessed=2 * padded * 2 * HD + 8 * rows * columns,
            transcendentals=rows * (columns // HD) * padded,
        ),
        compiler_params=pltpu.CompilerParams(vmem_limit_bytes=40 * 2**20),
        name="attend",
    )(span_map, order, mine, other, new_kv, positions[:, None], row_pos, *([payload] * CPR))


def output_kernel(plan, order_ref, half_ref, att_ref, *refs):
    count = 1 + max(copy[0] for copies in plan for copy in copies)
    sources = refs[:count]
    out_ref, w_buf, o_buf, in_sem, out_sem = refs[count:]
    slots = len(plan)
    third = w_buf.shape[3]
    loads = []
    for p, copies in enumerate(plan):
        group = []
        for n, (src, index, part, first, size) in enumerate(copies):
            view = sources[src] if index is None else sources[src].at[index]
            copy = pltpu.make_async_copy(
                view, w_buf.at[p, part, pl.ds(first, size)], in_sem.at[p, n]
            )
            copy.start()
            group.append(copy)
        loads.append(group)
    stores = []
    half = half_ref[0]
    for p in range(slots):
        for copy in loads[p]:
            copy.wait()
        own = p % CHIPS == 0
        for part in range(3):
            o_buf[p, part] = jnp.dot(
                att_ref[...], w_buf[p, part], preferred_element_type=jnp.float32
            ).astype(jnp.bfloat16)
            lot = (half, 2, 1 - half)[part] if not own else part
            start = pl.multiple_of(order_ref[p] * (3 * third) + lot * third, third)
            copy = pltpu.make_async_copy(
                o_buf.at[p, part], out_ref.at[0, :, pl.ds(start, third)], out_sem.at[p, part]
            )
            copy.start()
            stores.append(copy)
    for copy in stores:
        copy.wait()


def project_output(order, half, attended, plan, sources, depth, third):
    rows = attended.shape[0]
    slots = len(plan)
    most = max(len(copies) for copies in plan)
    width = slots * 3 * third
    return pl.pallas_call(
        partial(output_kernel, plan),
        grid_spec=pltpu.PrefetchScalarGridSpec(
            num_scalar_prefetch=2,
            grid=(1,),
            in_specs=[pl.BlockSpec((rows, depth), lambda i, *_: (0, 0))]
            + [pl.BlockSpec(memory_space=pl.ANY)] * len(sources),
            out_specs=pl.BlockSpec(memory_space=pl.ANY),
            scratch_shapes=[
                pltpu.VMEM((slots, 3, depth, third), jnp.bfloat16),
                pltpu.VMEM((slots, 3, rows, third), jnp.bfloat16),
                pltpu.SemaphoreType.DMA((slots, most)),
                pltpu.SemaphoreType.DMA((slots, 3)),
            ],
        ),
        out_shape=jax.ShapeDtypeStruct((1, rows, width), jnp.bfloat16),
        cost_estimate=pl.CostEstimate(
            flops=2 * rows * depth * width,
            bytes_accessed=2 * width * (rows + depth),
            transcendentals=0,
        ),
        compiler_params=pltpu.CompilerParams(vmem_limit_bytes=44 * 2**20),
        name="project_output",
    )(order, half, attended, *sources)


def gather_ring(block, split):
    ahead = back = block
    held = [block]
    for _ in range(CHIPS // 2 - 1):
        ahead, back = move(ahead, AHEAD), move(back, BACK)
        held += [ahead, back]
    first, second = split(ahead, back)
    return held, (move(first, AHEAD), move(second, BACK))


def ring_body(
    span_states,
    recomp_states,
    w_query,
    w_kv,
    w_out,
    span_map,
    span_lengths,
    recompute_idx,
    block_table,
):
    group = lax.axis_index("groups")
    width, heads, part = w_query.shape
    half = width // 2
    depth = heads * HD
    columns = w_out.shape[3]
    third = columns // 3
    slots = CHIPS * CORES
    order = jnp.asarray(slot_table())[lax.axis_index("serve")]
    group_arr = group.astype(jnp.int32)[None]

    theirs = lax.dynamic_slice_in_dim(recomp_states[0], (1 - group) * half, half, 1)
    other_rows = across(theirs)
    query_rows = w_query.transpose(1, 2, 0).reshape(heads * part, width)
    query_rows = lax.dynamic_slice_in_dim(query_rows, group * half, half, 1)
    kv_rows = w_kv.transpose(1, 2, 0).reshape(2 * part, width)
    block = jnp.concatenate([query_rows, kv_rows[:, :half], kv_rows[:, half:]], axis=0)
    cut = heads * part
    held, (far_query, far_kv) = gather_ring(block, lambda a, b: (a[:cut], b[cut:]))
    both = held + [move(b, SIBLING) for b in held]
    far_query = [far_query, move(far_query, SIBLING)]
    far_kv = [far_kv, move(far_kv, SIBLING)]

    payload, new_kv, cache = project_kv(
        order, block_table, span_lengths, span_states, recomp_states, both, far_kv
    )
    payloads = lax.all_gather(payload, "serve", axis=0)
    mine, theirs_part = project_query(group_arr, recomp_states, other_rows, both, far_query, depth)
    other = across(theirs_part)

    own_out = w_out.reshape(depth, columns)
    shared = lax.dynamic_slice_in_dim(own_out, group * third, third, 1)
    out_block = jnp.stack([shared, own_out[:, 2 * third :]])
    cut = depth // 2
    out_held, out_far = gather_ring(out_block, lambda a, b: (a[:, :cut], b[:, cut:]))
    ring_blocks = out_held[1:] + list(out_far)
    side_blocks = [across(b[0]) for b in ring_blocks]
    sources = [own_out, *ring_blocks, *side_blocks]
    sources += [move(b, SIBLING) for b in sources]
    step = len(sources) // CORES
    plan = []
    for c in range(CORES):
        at = c * step
        columns_of = lambda t: (slice(None), pl.ds(t * third, third))
        plan.append([(at, columns_of(t), t, 0, depth) for t in range(3)])
        for n in range(CHIPS - 2):
            ring_at, side_at = at + 1 + n, at + 1 + CHIPS + n
            plan.append(
                [(ring_at, 0, 0, 0, depth), (ring_at, 1, 1, 0, depth), (side_at, None, 2, 0, depth)]
            )
        far = []
        for n in range(2):
            ring_at, side_at = at + CHIPS - 1 + n, at + 2 * CHIPS - 1 + n
            far += [
                (ring_at, 0, 0, n * cut, cut),
                (ring_at, 1, 1, n * cut, cut),
                (side_at, None, 2, n * cut, cut),
            ]
        plan.append(far)

    attended = attend(span_map[0], order, mine, other, new_kv, recompute_idx[0], payloads)
    attn_out = project_output(order, group_arr, attended, plan, sources, depth, third)
    return (cache, attn_out)


def solution(mesh):
    in_specs = (
        P(("groups", "serve"), None, "tensor"),
        P(("groups", "serve"), None, "tensor"),
        P("tensor", None, "serve"),
        P("tensor", None, "serve"),
        P("tensor", None, None, "serve"),
        P(("groups", "serve"), None),
        P(("groups", "serve")),
        P(("groups", "serve"), None),
        P(("groups", "serve")),
    )
    out_specs = (P(("groups", "serve"), None, None), P(("groups", "serve"), None, "tensor"))
    body = ring_body if ring_fits(mesh) else general_body
    return jax.shard_map(body, mesh=mesh, in_specs=in_specs, out_specs=out_specs, check_vma=False)
```

```python
from functools import partial
import math

import jax
import jax.numpy as jnp
import numpy as np
from jax import lax
from jax.experimental import pallas as pl
from jax.experimental.pallas import tpu as pltpu
from jax.sharding import PartitionSpec as P

HD = 128
SPAN = 256
PAGE = 16
CPR = 6
PPC = 16


def merge_block(state, query, key_rows, value_rows, allowed, score_scale):
    old_max, old_sum, old_acc = state
    scores = (
        jnp.einsum("rhc,kc->rhk", query, key_rows, preferred_element_type=jnp.float32) * score_scale
    )
    block_max = jnp.max(jnp.where(allowed, scores, -jnp.inf), axis=2)
    new_max = jnp.maximum(old_max, block_max)
    weights_now = jnp.where(allowed, jnp.exp(scores - new_max[:, :, None]), 0.0)
    rescale = jnp.exp(old_max - new_max)
    new_acc = old_acc * rescale[:, :, None] + jnp.einsum(
        "rhk,kc->rhc", weights_now, value_rows.astype(jnp.float32)
    )
    return (new_max, old_sum * rescale + jnp.sum(weights_now, axis=2), new_acc)


def general_body(
    span_states,
    recomp_states,
    w_query,
    w_kv,
    w_out,
    span_map,
    span_lengths,
    recompute_idx,
    block_table,
):
    span_rows = span_states[0]
    req_rows = recomp_states[0]
    num_recomp = req_rows.shape[0]
    all_heads = w_query.shape[1]
    query_piece = lax.all_gather(w_query, "serve", axis=2, tiled=True)
    kv_piece = lax.all_gather(w_kv, "serve", axis=2, tiled=True)
    query_part = jnp.einsum(
        "rd,dhc->rhc", req_rows, query_piece, preferred_element_type=jnp.float32
    )
    new_part = jnp.einsum("rd,dhc->rhc", req_rows, kv_piece, preferred_element_type=jnp.float32)
    span_part = jnp.einsum("rd,dhc->rhc", span_rows, kv_piece, preferred_element_type=jnp.float32)
    query_full, new_full, span_full = lax.psum((query_part, new_part, span_part), "tensor")
    core_heads = all_heads // lax.axis_size("tensor")
    my_core = lax.axis_index("tensor")
    query = lax.dynamic_slice_in_dim(query_full, my_core * core_heads, core_heads, 1).astype(
        jnp.bfloat16
    )
    new_kv = new_full.astype(jnp.bfloat16)
    span_kv = span_full.astype(jnp.bfloat16)
    logical_pages = span_kv.reshape(PPC, PAGE, 2 * HD)
    inverse = jnp.argsort(block_table)
    physical = logical_pages[inverse]
    page_lens = jnp.repeat(span_lengths, PPC, total_repeat_length=PPC)
    positions = recompute_idx[0]
    my_spans = span_map[0]
    score_scale = HD ** (-0.5)
    slot_ids = jnp.arange(CPR, dtype=jnp.int32)
    token_ids = jnp.arange(PAGE, dtype=jnp.int32)
    local_allowed = (positions[None, :] <= positions[:, None])[:, None, :]
    empty_state = (
        jnp.full((num_recomp, core_heads), -jnp.inf, jnp.float32),
        jnp.zeros((num_recomp, core_heads), jnp.float32),
        jnp.zeros((num_recomp, core_heads, HD), jnp.float32),
    )
    state = merge_block(empty_state, query, new_kv[:, 0], new_kv[:, 1], local_allowed, score_scale)

    def block_update(skipping, totals, block):
        page_data, logical, lens_block, first_page = block
        width = page_data.shape[0]
        global_page = first_page + jnp.arange(width, dtype=jnp.int32)
        span_id = global_page // PPC
        matches = my_spans[None, :] == span_id[:, None]
        in_request = jnp.any(matches, axis=1)
        slot_num = jnp.sum(jnp.where(matches, slot_ids[None, :], 0), axis=1)
        offset = logical[:, None] * PAGE + token_ids[None, :]
        key_pos = (slot_num[:, None] * SPAN + offset).reshape(width * PAGE)
        usable = (in_request[:, None] & (offset < lens_block[:, None])).reshape(width * PAGE)
        redone = jnp.any(key_pos[:, None] == positions[None, :], axis=1)
        usable = usable & jnp.logical_not(redone)
        allowed = (usable[None, :] & (key_pos[None, :] <= positions[:, None]))[:, None, :]
        key_rows = page_data.reshape(width * PAGE, 2, HD)
        result = merge_block(totals, query, key_rows[:, 0], key_rows[:, 1], allowed, score_scale)
        return (result, None)

    page_data = lax.all_gather(physical, "serve", axis=0, tiled=True)
    logical = lax.all_gather(inverse, "serve", axis=0, tiled=True)
    lens_piece = lax.all_gather(page_lens, "serve", axis=0, tiled=True)
    count = page_data.shape[0]
    block = math.gcd(count, 64)
    steps_here = count // block
    blocks = (
        page_data.reshape(steps_here, block, PAGE, 2 * HD),
        logical.reshape(steps_here, block),
        lens_piece.reshape(steps_here, block),
        jnp.arange(steps_here, dtype=jnp.int32) * block,
    )
    result, unused_out = lax.scan(partial(block_update, False), state, blocks)
    state = result
    run_max, run_sum, run_acc = state
    attended = (run_acc / run_sum[:, :, None]).astype(jnp.bfloat16)
    partial_out = jnp.einsum(
        "rhc,hctd->rtd",
        attended,
        lax.all_gather(w_out, "serve", axis=3, tiled=True),
        preferred_element_type=jnp.float32,
    )
    reduced = lax.psum_scatter(
        partial_out.astype(jnp.bfloat16), "tensor", scatter_dimension=1, tiled=True
    )
    attn_out = reduced.reshape(1, reduced.shape[0], reduced.shape[2])
    return (physical, attn_out)


CHIPS = 8
CORES = 2
RING = ((0, 0), (1, 0), (2, 0), (3, 0), (3, 1), (2, 1), (1, 1), (0, 1))
CHIP_AT = tuple((z * 2 + y) * CORES for z, y in RING)
NT = (((1,), (1,)), ((), ()))


def ring_fits(mesh):
    return tuple(mesh.shape[name] for name in ("groups", "serve", "tensor")) == (2, CHIPS * CORES, 1)


def ring_pairs(step):
    return [
        (CHIP_AT[i] + c, CHIP_AT[(i + step) % CHIPS] + c) for i in range(CHIPS) for c in range(CORES)
    ]


AHEAD, BACK = ring_pairs(1), ring_pairs(-1)
SIBLING = [(i, i ^ 1) for i in range(CHIPS * CORES)]
ACROSS = [(0, 1), (1, 0)]


def slot_table():
    table = np.zeros((CHIPS * CORES, CHIPS * CORES), np.int32)
    for i in range(CHIPS):
        for c in range(CORES):
            for slot, step in enumerate((0, -1, 1, -2, 2, -3, 3, 4)):
                chip = CHIP_AT[(i + step) % CHIPS]
                table[CHIP_AT[i] + c, slot] = chip + c
                table[CHIP_AT[i] + c, CHIPS + slot] = chip + 1 - c
    return table


def in_hbm(blocks):
    return [pltpu.with_memory_space_constraint(block, pltpu.HBM) for block in blocks]


def in_vmem(blocks):
    return [pltpu.with_memory_space_constraint(block, pltpu.VMEM) for block in blocks]


def hold_kernel(packs, *refs):
    for pack, out_ref in zip(packs, refs[len(refs) - len(packs) :]):
        at = 0
        for n, first, size in pack:
            out_ref[at : at + size] = refs[n][first : first + size]
            at += size


def together(*blocks, packs=()):
    read = [n for pack in packs for n, first, size in pack]
    packed = [
        (sum(size for n, first, size in pack),) + blocks[pack[0][0]].shape[1:] for pack in packs
    ]
    return pl.pallas_call(
        partial(hold_kernel, packs),
        in_specs=[
            pl.BlockSpec(memory_space=pltpu.VMEM if n in read else pl.ANY) for n in range(len(blocks))
        ],
        out_specs=[pl.BlockSpec(memory_space=pl.ANY)] * len(blocks)
        + [pl.BlockSpec(memory_space=pltpu.VMEM)] * len(packs),
        out_shape=[pltpu.VMEM(block.shape, block.dtype) for block in blocks]
        + [pltpu.VMEM(shape, jnp.bfloat16) for shape in packed],
        input_output_aliases={n: n for n in range(len(blocks))},
        compiler_params=pltpu.CompilerParams(vmem_limit_bytes=2**20),
        name="together",
    )(*in_vmem(blocks))


def copy_kernel(plan, facts, *refs):
    sem = refs[-1]
    group = facts[GROUP]
    copies = []
    for n, (source, out, row, first, flip, shape) in enumerate(plan):
        side = 1 - group if flip else group
        width = shape[-1]
        start = first if flip is None else pl.multiple_of(side * width, width)
        view = refs[source].at[pl.ds(row[0], shape[0]), pl.ds(start, width)]
        copies.append(
            pltpu.make_async_copy(view, refs[out].at[pl.ds(row[1], shape[0])], sem.at[n])
        )
    for copy in copies:
        copy.start()
    for copy in copies:
        copy.wait()


def take_parts(facts, sources, outs, plan):
    count = len(sources)
    plan = [(s, count + o, *rest) for s, o, *rest in plan]
    return pl.pallas_call(
        partial(copy_kernel, plan),
        grid_spec=pltpu.PrefetchScalarGridSpec(
            num_scalar_prefetch=1,
            grid=(),
            in_specs=[pl.BlockSpec(memory_space=pl.ANY)] * count,
            out_specs=[pl.BlockSpec(memory_space=pltpu.VMEM)] * len(outs),
            scratch_shapes=[pltpu.SemaphoreType.DMA((len(plan),))],
        ),
        out_shape=[pltpu.VMEM(shape, jnp.bfloat16) for shape in outs],
        compiler_params=pltpu.CompilerParams(vmem_limit_bytes=2**20),
        name="take_parts",
    )(facts, *in_hbm(sources))


def move(block, pairs):
    return lax.ppermute(block, "serve", pairs)


def across(block):
    return lax.ppermute(block, "groups", ACROSS)


GROUP, LENGTH, ORDER, TABLE = 0, 1, 2, 2 + CHIPS * CORES


def column_order(facts, slots, planes):
    rows, width = planes * 8, planes * HD
    row = lax.broadcasted_iota(jnp.int32, (rows, width), 0)
    col = lax.broadcasted_iota(jnp.int32, (rows, width), 1)
    place = (row // 8) * HD + row % 8
    parts = [(col == place + facts[ORDER + p] * 8).astype(jnp.float32) for p in range(slots)]
    return jnp.concatenate(parts, axis=0).astype(jnp.bfloat16)


def kv_kernel(facts, span_ref, req_ref, *refs):
    slots = CHIPS * CORES
    w_refs = refs[:slots]
    pay_ref, new_ref, cache_ref, span_acc, req_acc = refs[slots:]
    step = pl.program_id(0)
    chunk = span_ref.shape[2]
    per_half = w_refs[0].shape[1] // chunk
    columns = pl.ds(pl.multiple_of(step % per_half * chunk, chunk), chunk)
    w = jnp.concatenate(
        [
            ref[pl.ds(pl.multiple_of(ref.shape[0] - 32 + step // per_half * 16, 16), 16), columns]
            for ref in w_refs
        ],
        axis=0,
    )
    span_now = lax.dot_general(span_ref[0], w, NT, preferred_element_type=jnp.float32)
    req_now = lax.dot_general(req_ref[0], w, NT, preferred_element_type=jnp.float32)

    @pl.when(step == 0)
    def _():
        span_acc[...] = span_now
        req_acc[...] = req_now

    @pl.when(step > 0)
    def _():
        span_acc[...] += span_now
        req_acc[...] += req_now

    @pl.when(step == pl.num_programs(0) - 1)
    def _():
        order = column_order(facts, slots, 2)
        span_kv = jnp.dot(
            span_acc[...].astype(jnp.bfloat16), order, preferred_element_type=jnp.float32
        ).astype(jnp.bfloat16)
        new_ref[...] = jnp.dot(
            req_acc[...].astype(jnp.bfloat16), order, preferred_element_type=jnp.float32
        ).astype(jnp.bfloat16)
        tokens = span_kv.shape[0]
        pay_ref[0:tokens] = span_kv
        length = jnp.full((PAGE, 2 * HD), facts[LENGTH], jnp.int32)
        pay_ref[tokens:] = length.astype(jnp.float32).astype(jnp.bfloat16)
        for p in range(tokens // PAGE):
            cache_ref[facts[TABLE + p]] = span_kv[p * PAGE : (p + 1) * PAGE]


def project_kv(facts, span_states, recomp_states, w_blocks, last_block):
    tokens, width = span_states.shape[1:]
    rows = recomp_states.shape[1]
    chunk = width // 4
    blocks = w_blocks[: CHIPS - 1] + last_block[:1] + w_blocks[CHIPS - 1 :] + last_block[1:]
    return pl.pallas_call(
        kv_kernel,
        grid_spec=pltpu.PrefetchScalarGridSpec(
            num_scalar_prefetch=1,
            grid=(width // chunk,),
            in_specs=[
                pl.BlockSpec((1, tokens, chunk), lambda k, *_: (0, 0, k)),
                pl.BlockSpec((1, rows, chunk), lambda k, *_: (0, 0, k)),
                *([pl.BlockSpec(memory_space=pltpu.VMEM)] * len(blocks)),
            ],
            out_specs=[
                pl.BlockSpec((tokens + PAGE, 2 * HD), lambda k, *_: (0, 0)),
                pl.BlockSpec((rows, 2 * HD), lambda k, *_: (0, 0)),
                pl.BlockSpec((tokens // PAGE, PAGE, 2 * HD), lambda k, *_: (0, 0, 0)),
            ],
            scratch_shapes=[
                pltpu.VMEM((tokens, 2 * HD), jnp.float32),
                pltpu.VMEM((rows, 2 * HD), jnp.float32),
            ],
        ),
        out_shape=[
            jax.ShapeDtypeStruct((tokens + PAGE, 2 * HD), jnp.bfloat16),
            jax.ShapeDtypeStruct((rows, 2 * HD), jnp.bfloat16),
            jax.ShapeDtypeStruct((tokens // PAGE, PAGE, 2 * HD), jnp.bfloat16),
        ],
        cost_estimate=pl.CostEstimate(
            flops=2 * (tokens + rows) * width * 2 * HD,
            bytes_accessed=2 * (tokens + rows + 2 * HD) * width,
            transcendentals=0,
        ),
        compiler_params=pltpu.CompilerParams(vmem_limit_bytes=16 * 2**20),
        name="project_kv",
    )(facts, *in_hbm([span_states, recomp_states]), *blocks)


def query_kernel(facts, mine_ref, *refs):
    slots = CHIPS * CORES
    w_refs = refs[:slots]
    other_refs = refs[slots:-4]
    mine_out, other_out, mine_acc, other_acc = refs[-4:]
    step = pl.program_id(0)
    chunk = mine_ref.shape[2]
    part = mine_out.shape[1] // slots
    columns = pl.ds(pl.multiple_of(step * chunk, chunk), chunk)
    w = jnp.concatenate([ref[0:part, columns] for ref in w_refs], axis=0)
    mine_now = lax.dot_general(mine_ref[0], w, NT, preferred_element_type=jnp.float32)
    other = jnp.concatenate([ref[:, columns] for ref in other_refs], axis=0)
    other_now = lax.dot_general(other, w, NT, preferred_element_type=jnp.float32)

    @pl.when(step == 0)
    def _():
        mine_acc[...] = mine_now
        other_acc[...] = other_now

    @pl.when(step > 0)
    def _():
        mine_acc[...] += mine_now
        other_acc[...] += other_now

    @pl.when(step == pl.num_programs(0) - 1)
    def _():
        mine_out[...] = mine_acc[...]
        other_out[...] = other_acc[...].astype(other_out.dtype)


def project_query(facts, recomp_states, other_rows, w_blocks, last_block, columns):
    rows = recomp_states.shape[1]
    depth = other_rows[0].shape[1]
    chunk = depth // 6
    steps = depth // chunk
    blocks = w_blocks[: CHIPS - 1] + last_block[:1] + w_blocks[CHIPS - 1 :] + last_block[1:]
    return pl.pallas_call(
        query_kernel,
        grid_spec=pltpu.PrefetchScalarGridSpec(
            num_scalar_prefetch=1,
            grid=(steps,),
            in_specs=[
                pl.BlockSpec((1, rows, chunk), lambda k, facts: (0, 0, facts[GROUP] * steps + k)),
                *([pl.BlockSpec(memory_space=pltpu.VMEM)] * (len(blocks) + len(other_rows))),
            ],
            out_specs=[
                pl.BlockSpec((rows, columns), lambda k, *_: (0, 0)),
                pl.BlockSpec((rows, columns), lambda k, *_: (0, 0)),
            ],
            scratch_shapes=[
                pltpu.VMEM((rows, columns), jnp.float32),
                pltpu.VMEM((rows, columns), jnp.float32),
            ],
        ),
        out_shape=[
            jax.ShapeDtypeStruct((rows, columns), jnp.float32),
            jax.ShapeDtypeStruct((rows, columns), jnp.bfloat16),
        ],
        cost_estimate=pl.CostEstimate(
            flops=4 * rows * depth * columns,
            bytes_accessed=2 * (2 * rows + columns) * depth,
            transcendentals=0,
        ),
        compiler_params=pltpu.CompilerParams(vmem_limit_bytes=16 * 2**20),
        name="project_query",
    )(facts, *in_hbm([recomp_states]), *blocks, *other_rows)


def attend_kernel(map_ref, facts, mine_ref, other_ref, new_ref, row_ref, *refs):
    span_refs = refs[:CPR]
    out_ref, keys, values, bias = refs[CPR:]
    rows = new_ref.shape[0]
    cached = CPR * SPAN
    padded = keys.shape[0]
    for s in range(CPR):
        keys[s * SPAN : (s + 1) * SPAN] = span_refs[s][0, 0:SPAN, 0:HD]
        values[s * SPAN : (s + 1) * SPAN] = span_refs[s][0, 0:SPAN, HD : 2 * HD]
    keys[cached : cached + rows] = new_ref[:, 0:HD]
    values[cached : cached + rows] = new_ref[:, HD : 2 * HD]
    keys[cached + rows :] = jnp.zeros((padded - cached - rows, HD), jnp.bfloat16)
    values[cached + rows :] = jnp.zeros((padded - cached - rows, HD), jnp.bfloat16)
    new_pos = jnp.broadcast_to(row_ref[...], (rows, rows))
    diagonal = lax.broadcasted_iota(jnp.int32, (rows, rows), 0) == lax.broadcasted_iota(
        jnp.int32, (rows, rows), 1
    )
    mine_at = jnp.sum(jnp.where(diagonal, new_pos, 0), axis=1, keepdims=True)
    new_allowed = new_pos <= jnp.broadcast_to(mine_at, (rows, rows))
    mine_at = jnp.broadcast_to(mine_at, (rows, SPAN))
    lane = lax.broadcasted_iota(jnp.int32, (rows, SPAN), 1)
    blocked = jnp.float32(-jnp.inf)
    for s in range(CPR):
        key_pos = lane + s * SPAN
        redone = jnp.max(jnp.where(mine_at == key_pos, 1.0, 0.0), axis=0, keepdims=True)
        length = span_refs[s][0, SPAN : SPAN + PAGE, :].astype(jnp.float32)[0:1]
        offset = lax.broadcasted_iota(jnp.int32, (1, SPAN), 1).astype(jnp.float32)
        usable = jnp.where(offset < length, 1.0 - redone, 0.0)
        allowed = (jnp.broadcast_to(usable, (rows, SPAN)) > 0.5) & (key_pos <= mine_at)
        bias[:, s * SPAN : (s + 1) * SPAN] = jnp.where(allowed, 0.0, blocked)
    bias[:, cached:] = jnp.full((rows, padded - cached), blocked, jnp.float32)
    bias[:, cached : cached + rows] = jnp.where(new_allowed, 0.0, blocked)

    query = (mine_ref[...] + other_ref[...].astype(jnp.float32)).astype(jnp.bfloat16)
    heads = query.shape[1] // HD
    order = column_order(facts, CHIPS * CORES, heads)
    query = jnp.dot(query, order, preferred_element_type=jnp.float32).astype(jnp.bfloat16)
    for h in range(heads):
        scores = lax.dot_general(
            query[:, h * HD : (h + 1) * HD], keys[...], NT, preferred_element_type=jnp.float32
        )
        scores = scores * (HD ** (-0.5)) + bias[...]
        top = jnp.max(scores, axis=1, keepdims=True)
        weights = jnp.exp(scores - top)
        total = jnp.sum(weights, axis=1, keepdims=True)
        mixed = jnp.dot(weights.astype(jnp.bfloat16), values[...], preferred_element_type=jnp.float32)
        out_ref[:, h * HD : (h + 1) * HD] = (mixed / total).astype(jnp.bfloat16)


def attend(span_map, facts, mine, other, new_kv, positions, payload):
    rows, columns = mine.shape
    cached = CPR * SPAN
    padded = cached + SPAN
    whole = lambda *shape: pl.BlockSpec(shape, lambda i, *_: (0,) * len(shape))
    slot = lambda s: pl.BlockSpec((1,) + payload.shape[1:], lambda i, map_ref, *_: (map_ref[s], 0, 0))
    return pl.pallas_call(
        attend_kernel,
        grid_spec=pltpu.PrefetchScalarGridSpec(
            num_scalar_prefetch=2,
            grid=(1,),
            in_specs=[
                whole(rows, columns),
                whole(rows, columns),
                whole(rows, 2 * HD),
                whole(1, rows),
                *[slot(s) for s in range(CPR)],
            ],
            out_specs=whole(rows, columns),
            scratch_shapes=[
                pltpu.VMEM((padded, HD), jnp.bfloat16),
                pltpu.VMEM((padded, HD), jnp.bfloat16),
                pltpu.VMEM((rows, padded), jnp.float32),
            ],
        ),
        out_shape=jax.ShapeDtypeStruct((rows, columns), jnp.bfloat16),
        cost_estimate=pl.CostEstimate(
            flops=4 * rows * columns * padded,
            bytes_accessed=2 * padded * 2 * HD + 8 * rows * columns,
            transcendentals=rows * (columns // HD) * padded,
        ),
        compiler_params=pltpu.CompilerParams(vmem_limit_bytes=20 * 2**20),
        name="attend",
    )(span_map, facts, mine, other, new_kv, positions, *in_hbm([payload] * CPR))


def output_kernel(plan, arrived, facts, att_ref, att2_ref, *refs):
    out_ref, sent_ref, w_buf, o_buf, in_sem, out_sem, late_sem = refs[-7:]
    third = o_buf.shape[3]
    rows = o_buf.shape[2]
    loads = []
    for p, (slot, lots) in enumerate(plan):
        copies = []
        for lot, parts in enumerate(lots):
            for n, (source, row, column, first, size) in enumerate(parts):
                view = refs[source].at[pl.ds(row, size), pl.ds(column, third)]
                copies.append(
                    pltpu.make_async_copy(
                        view, w_buf.at[p, lot, pl.ds(first, size)], in_sem.at[p, lot, n]
                    )
                )
        for copy in copies:
            copy.start()
        loads.append(copies)
    stores = place(facts, [(refs[source], slots) for source, slots in arrived], out_ref, late_sem)
    attended = jnp.concatenate([att_ref[...], att2_ref[...]], axis=0)
    for p, (slot, lots) in enumerate(plan):
        for copy in loads[p]:
            copy.wait()
        for lot in range(len(lots)):
            both = jnp.dot(
                attended, w_buf[p, lot], preferred_element_type=jnp.float32
            ).astype(jnp.bfloat16)
            o_buf[p, lot] = both[:rows]
            sent_ref[p, lot] = both[rows:]
            copy = pltpu.make_async_copy(
                o_buf.at[p, lot],
                out_ref.at[0, :, pl.ds(place_of(facts, slot, lot, third), third)],
                out_sem.at[p, lot],
            )
            copy.start()
            stores.append(copy)
    for copy in stores:
        copy.wait()


def place_of(facts, slot, lot, third):
    group = facts[GROUP]
    kind = lot if slot % CHIPS == 0 else (group, 2, 1 - group)[lot]
    return pl.multiple_of(facts[ORDER + slot] * (3 * third) + kind * third, third)


def place(facts, arrived, out_ref, sem):
    copies = []
    for ref, slots in arrived:
        third = ref.shape[3]
        for p, slot in enumerate(slots):
            for lot in range(3):
                start = place_of(facts, slot + CHIPS, lot, third)
                copy = pltpu.make_async_copy(
                    ref.at[p, lot], out_ref.at[0, :, pl.ds(start, third)], sem.at[len(copies)]
                )
                copy.start()
                copies.append(copy)
    return copies


def place_kernel(slots, facts, *refs):
    before_ref, out_ref, sem = refs[-3:]
    for copy in place(facts, list(zip(refs, slots)), out_ref, sem):
        copy.wait()


def place_output(facts, arrived, before):
    blocks = [block for block, _ in arrived]
    slots = [slots for _, slots in arrived]
    return pl.pallas_call(
        partial(place_kernel, slots),
        grid_spec=pltpu.PrefetchScalarGridSpec(
            num_scalar_prefetch=1,
            grid=(),
            in_specs=[pl.BlockSpec(memory_space=pl.ANY)] * (len(blocks) + 1),
            out_specs=pl.BlockSpec(memory_space=pl.ANY),
            scratch_shapes=[pltpu.SemaphoreType.DMA((3 * sum(map(len, slots)),))],
        ),
        out_shape=pltpu.HBM(before.shape, jnp.bfloat16),
        input_output_aliases={1 + len(blocks): 0},
        compiler_params=pltpu.CompilerParams(vmem_limit_bytes=2**20),
        name="place_output",
    )(facts, *blocks, *in_hbm([before]))


def project_output(facts, attended, before, work, arrived, width):
    rows, depth = attended[0].shape
    sources = []

    def index_of(block):
        if not any(block is held for held in sources):
            sources.append(block)
        return [block is held for held in sources].index(True)

    plan = [
        (slot, [[(index_of(block), *where) for block, *where in lot] for lot in lots])
        for slot, lots in work
    ]
    arrived = [(index_of(block), slots) for block, slots in arrived]
    placed = 3 * sum(len(slots) for _, slots in arrived)
    third = width // (CHIPS * CORES * 3)
    filled = [] if before is None else [before]
    return pl.pallas_call(
        partial(output_kernel, plan, arrived),
        grid_spec=pltpu.PrefetchScalarGridSpec(
            num_scalar_prefetch=1,
            grid=(),
            in_specs=[pl.BlockSpec(memory_space=pltpu.VMEM)] * CORES
            + [pl.BlockSpec(memory_space=pl.ANY)] * (len(sources) + len(filled)),
            out_specs=[pl.BlockSpec(memory_space=pl.ANY), pl.BlockSpec(memory_space=pltpu.VMEM)],
            scratch_shapes=[
                pltpu.VMEM((len(plan), 3, depth, third), jnp.bfloat16),
                pltpu.VMEM((len(plan), 3, rows, third), jnp.bfloat16),
                pltpu.SemaphoreType.DMA((len(plan), 3, 2)),
                pltpu.SemaphoreType.DMA((len(plan), 3)),
                pltpu.SemaphoreType.DMA((max(placed, 1),)),
            ],
        ),
        out_shape=[
            pltpu.HBM((1, rows, width), jnp.bfloat16),
            pltpu.VMEM((len(plan), 3, rows, third), jnp.bfloat16),
        ],
        input_output_aliases={1 + CORES + len(sources): 0} if filled else {},
        cost_estimate=pl.CostEstimate(
            flops=2 * rows * CORES * depth * 3 * third * len(plan),
            bytes_accessed=2 * 3 * third * len(plan) * (rows + depth),
            transcendentals=0,
        ),
        compiler_params=pltpu.CompilerParams(vmem_limit_bytes=(len(plan) * 3 + 6) * 2**20),
        name="project_output",
    )(facts, *attended, *sources, *in_hbm(filled))


def ring_body(
    span_states,
    recomp_states,
    w_query,
    w_kv,
    w_out,
    span_map,
    span_lengths,
    recompute_idx,
    block_table,
):
    swap = lambda *blocks: tuple(move(block, SIBLING) for block in blocks)
    group = lax.axis_index("groups")
    width, heads, part = w_query.shape
    rows = recomp_states.shape[1]
    half = width // 2
    depth = heads * HD
    columns = w_out.shape[3]
    third = columns // 3
    order = jnp.asarray(slot_table())[lax.axis_index("serve")]
    facts = jnp.concatenate([group[None].astype(jnp.int32), span_lengths, order, block_table])

    query_rows = w_query.transpose(1, 2, 0).reshape(heads * part, width)
    kv_rows = w_kv.transpose(1, 2, 0).reshape(2 * part, width)
    own_out = w_out.reshape(depth, columns)
    lot = rows // 3
    cut = heads * part
    (block,) = take_parts(
        facts,
        [query_rows, kv_rows],
        [(cut + 4 * part, half)],
        [
            (0, 0, (0, 0), 0, False, (cut, half)),
            (1, 0, (0, cut), 0, None, (2 * part, half)),
            (1, 0, (0, cut + 2 * part), half, None, (2 * part, half)),
        ],
    )
    *theirs, out_block = take_parts(
        facts,
        [recomp_states[0], own_out, block],
        [(lot, half)] * 3 + [(2 * depth, third)],
        [(0, n, (n * lot, 0), 0, True, (lot, half)) for n in range(3)]
        + [
            (1, 3, (0, 0), 0, False, (depth, third)),
            (1, 3, (0, depth), 2 * third, None, (depth, third)),
        ],
    )
    out = (move(block, AHEAD), move(block, BACK), across(theirs[0]), *swap(block))
    ahead1, back1, rows1, block2 = together(*out)
    out = (move(ahead1, AHEAD), move(back1, BACK), across(theirs[1]), *swap(ahead1, back1))
    ahead2, back2, rows2, *swapped1 = together(*out)
    out = (move(ahead2, AHEAD), move(back2, BACK), across(theirs[2]), *swap(ahead2, back2))
    ahead3, back3, rows3, *swapped2, to_ahead, to_back = together(
        *out, packs=([(0, 0, cut)], [(1, cut, 4 * part)])
    )
    far_query, far_kv, out_block, *swapped3 = together(
        move(to_ahead, AHEAD), move(to_back, BACK), out_block, *swap(ahead3, back3)
    )
    far_query2, far_kv2 = swap(far_query, far_kv)
    both = [block, ahead1, back1, ahead2, back2, ahead3, back3, block2, *swapped1, *swapped2, *swapped3]

    shared = lambda n: (n, 0, depth)
    payload, new_kv, cache = project_kv(
        facts, span_states, recomp_states, both, [far_kv, far_kv2]
    )
    mine, theirs_part = project_query(
        facts, recomp_states, (rows1, rows2, rows3), both, [far_query, far_query2], depth
    )
    a1, b1, payload, theirs_part = lax.optimization_barrier(
        (move(out_block, AHEAD), move(out_block, BACK), payload, theirs_part)
    )
    a1, b1, send1 = together(a1, b1, packs=([shared(0), shared(1)],))
    payloads = lax.all_gather(payload, "serve", axis=0)
    a2, b2, x1, send2 = together(
        move(a1, AHEAD), move(b1, BACK), across(send1), packs=([shared(0), shared(1)],)
    )
    cut = depth // 2
    a3, b3, x2, other, send3, to_ahead, to_back = together(
        move(a2, AHEAD),
        move(b2, BACK),
        across(send2),
        across(theirs_part),
        packs=(
            [shared(0), shared(1)],
            [(0, 0, cut), (0, depth, cut)],
            [(1, cut, cut), (1, depth + cut, cut)],
        ),
    )
    attended = attend(span_map[0], facts, mine, other, new_kv, recompute_idx, payloads)
    attended = (attended, *swap(attended))

    def near(slot, block, side, first):
        return slot, [
            [(block, 0, 0, 0, depth)],
            [(block, depth, 0, 0, depth)],
            [(side, first * depth, 0, 0, depth)],
        ]

    early = [
        (0, [[(own_out, 0, n * third, 0, depth)] for n in range(3)]),
        near(1, a1, x1, 0),
        near(2, b1, x1, 1),
        near(3, a2, x2, 0),
        near(4, b2, x2, 1),
    ]
    width_out = CHIPS * CORES * columns
    result, sent1 = project_output(facts, attended, None, early, [], width_out)
    a4, b4, x3, sent1 = lax.optimization_barrier(
        (move(to_ahead, AHEAD), move(to_back, BACK), across(send3), sent1)
    )
    a4, b4, x3, send4 = together(a4, b4, x3, packs=([(0, 0, cut), (1, 0, cut)],))
    late = [near(5, a3, x3, 0), near(6, b3, x3, 1)]
    result, sent2 = project_output(facts, attended, result, late, [], width_out)
    x4, arrived1, sent2 = lax.optimization_barrier((across(send4), *swap(sent1), sent2))
    last = [
        (
            7,
            [
                [(a4, 0, 0, 0, cut), (b4, 0, 0, cut, cut)],
                [(a4, cut, 0, 0, cut), (b4, cut, 0, cut, cut)],
                [(x4, 0, 0, 0, depth)],
            ],
        )
    ]
    arrived = [(arrived1, (0, 1, 2, 3, 4))]
    result, sent3 = project_output(facts, attended, result, last, arrived, width_out)
    arrived = [(swap(sent2)[0], (5, 6)), (swap(sent3)[0], (7,))]
    return (cache, place_output(facts, arrived, result))


def solution(mesh):
    in_specs = (
        P(("groups", "serve"), None, "tensor"),
        P(("groups", "serve"), None, "tensor"),
        P("tensor", None, "serve"),
        P("tensor", None, "serve"),
        P("tensor", None, None, "serve"),
        P(("groups", "serve"), None),
        P(("groups", "serve")),
        P(("groups", "serve"), None),
        P(("groups", "serve")),
    )
    out_specs = (P(("groups", "serve"), None, None), P(("groups", "serve"), None, "tensor"))
    body = ring_body if ring_fits(mesh) else general_body
    return jax.shard_map(body, mesh=mesh, in_specs=in_specs, out_specs=out_specs, check_vma=False)
```

```python
from functools import partial
import math

import jax
import jax.numpy as jnp
import numpy as np
from jax import lax
from jax.experimental import pallas as pl
from jax.experimental.pallas import tpu as pltpu
from jax.sharding import PartitionSpec as P

HD = 128
SPAN = 256
PAGE = 16
CPR = 6
PPC = 16


def merge_block(state, query, key_rows, value_rows, allowed, score_scale):
    old_max, old_sum, old_acc = state
    scores = (
        jnp.einsum("rhc,kc->rhk", query, key_rows, preferred_element_type=jnp.float32) * score_scale
    )
    block_max = jnp.max(jnp.where(allowed, scores, -jnp.inf), axis=2)
    new_max = jnp.maximum(old_max, block_max)
    weights_now = jnp.where(allowed, jnp.exp(scores - new_max[:, :, None]), 0.0)
    rescale = jnp.exp(old_max - new_max)
    new_acc = old_acc * rescale[:, :, None] + jnp.einsum(
        "rhk,kc->rhc", weights_now, value_rows.astype(jnp.float32)
    )
    return (new_max, old_sum * rescale + jnp.sum(weights_now, axis=2), new_acc)


def general_body(
    span_states,
    recomp_states,
    w_query,
    w_kv,
    w_out,
    span_map,
    span_lengths,
    recompute_idx,
    block_table,
):
    span_rows = span_states[0]
    req_rows = recomp_states[0]
    num_recomp = req_rows.shape[0]
    all_heads = w_query.shape[1]
    query_piece = lax.all_gather(w_query, "serve", axis=2, tiled=True)
    kv_piece = lax.all_gather(w_kv, "serve", axis=2, tiled=True)
    query_part = jnp.einsum(
        "rd,dhc->rhc", req_rows, query_piece, preferred_element_type=jnp.float32
    )
    new_part = jnp.einsum("rd,dhc->rhc", req_rows, kv_piece, preferred_element_type=jnp.float32)
    span_part = jnp.einsum("rd,dhc->rhc", span_rows, kv_piece, preferred_element_type=jnp.float32)
    query_full, new_full, span_full = lax.psum((query_part, new_part, span_part), "tensor")
    core_heads = all_heads // lax.axis_size("tensor")
    my_core = lax.axis_index("tensor")
    query = lax.dynamic_slice_in_dim(query_full, my_core * core_heads, core_heads, 1).astype(
        jnp.bfloat16
    )
    new_kv = new_full.astype(jnp.bfloat16)
    span_kv = span_full.astype(jnp.bfloat16)
    logical_pages = span_kv.reshape(PPC, PAGE, 2 * HD)
    inverse = jnp.argsort(block_table)
    physical = logical_pages[inverse]
    page_lens = jnp.repeat(span_lengths, PPC, total_repeat_length=PPC)
    positions = recompute_idx[0]
    my_spans = span_map[0]
    score_scale = HD ** (-0.5)
    slot_ids = jnp.arange(CPR, dtype=jnp.int32)
    token_ids = jnp.arange(PAGE, dtype=jnp.int32)
    local_allowed = (positions[None, :] <= positions[:, None])[:, None, :]
    empty_state = (
        jnp.full((num_recomp, core_heads), -jnp.inf, jnp.float32),
        jnp.zeros((num_recomp, core_heads), jnp.float32),
        jnp.zeros((num_recomp, core_heads, HD), jnp.float32),
    )
    state = merge_block(empty_state, query, new_kv[:, 0], new_kv[:, 1], local_allowed, score_scale)

    def block_update(skipping, totals, block):
        page_data, logical, lens_block, first_page = block
        width = page_data.shape[0]
        global_page = first_page + jnp.arange(width, dtype=jnp.int32)
        span_id = global_page // PPC
        matches = my_spans[None, :] == span_id[:, None]
        in_request = jnp.any(matches, axis=1)
        slot_num = jnp.sum(jnp.where(matches, slot_ids[None, :], 0), axis=1)
        offset = logical[:, None] * PAGE + token_ids[None, :]
        key_pos = (slot_num[:, None] * SPAN + offset).reshape(width * PAGE)
        usable = (in_request[:, None] & (offset < lens_block[:, None])).reshape(width * PAGE)
        redone = jnp.any(key_pos[:, None] == positions[None, :], axis=1)
        usable = usable & jnp.logical_not(redone)
        allowed = (usable[None, :] & (key_pos[None, :] <= positions[:, None]))[:, None, :]
        key_rows = page_data.reshape(width * PAGE, 2, HD)
        result = merge_block(totals, query, key_rows[:, 0], key_rows[:, 1], allowed, score_scale)
        return (result, None)

    page_data = lax.all_gather(physical, "serve", axis=0, tiled=True)
    logical = lax.all_gather(inverse, "serve", axis=0, tiled=True)
    lens_piece = lax.all_gather(page_lens, "serve", axis=0, tiled=True)
    count = page_data.shape[0]
    block = math.gcd(count, 64)
    steps_here = count // block
    blocks = (
        page_data.reshape(steps_here, block, PAGE, 2 * HD),
        logical.reshape(steps_here, block),
        lens_piece.reshape(steps_here, block),
        jnp.arange(steps_here, dtype=jnp.int32) * block,
    )
    result, unused_out = lax.scan(partial(block_update, False), state, blocks)
    state = result
    run_max, run_sum, run_acc = state
    attended = (run_acc / run_sum[:, :, None]).astype(jnp.bfloat16)
    partial_out = jnp.einsum(
        "rhc,hctd->rtd",
        attended,
        lax.all_gather(w_out, "serve", axis=3, tiled=True),
        preferred_element_type=jnp.float32,
    )
    reduced = lax.psum_scatter(
        partial_out.astype(jnp.bfloat16), "tensor", scatter_dimension=1, tiled=True
    )
    attn_out = reduced.reshape(1, reduced.shape[0], reduced.shape[2])
    return (physical, attn_out)


CHIPS = 8
CORES = 2
RING = ((0, 0), (1, 0), (2, 0), (3, 0), (3, 1), (2, 1), (1, 1), (0, 1))
CHIP_AT = tuple((z * 2 + y) * CORES for z, y in RING)
NT = (((1,), (1,)), ((), ()))


def ring_fits(mesh):
    return tuple(mesh.shape[name] for name in ("groups", "serve", "tensor")) == (2, CHIPS * CORES, 1)


def ring_pairs(step):
    return [
        (CHIP_AT[i] + c, CHIP_AT[(i + step) % CHIPS] + c) for i in range(CHIPS) for c in range(CORES)
    ]


AHEAD, BACK = ring_pairs(1), ring_pairs(-1)
SIBLING = [(i, i ^ 1) for i in range(CHIPS * CORES)]
ACROSS = [(0, 1), (1, 0)]


def slot_table():
    table = np.zeros((CHIPS * CORES, CHIPS * CORES), np.int32)
    for i in range(CHIPS):
        for c in range(CORES):
            for slot, step in enumerate((0, -1, 1, -2, 2, -3, 3, 4)):
                chip = CHIP_AT[(i + step) % CHIPS]
                table[CHIP_AT[i] + c, slot] = chip + c
                table[CHIP_AT[i] + c, CHIPS + slot] = chip + 1 - c
    return table


def in_hbm(blocks):
    return [pltpu.with_memory_space_constraint(block, pltpu.HBM) for block in blocks]


def in_vmem(blocks):
    return [pltpu.with_memory_space_constraint(block, pltpu.VMEM) for block in blocks]


def hold_kernel(packs, *refs):
    for pack, out_ref in zip(packs, refs[len(refs) - len(packs) :]):
        at = 0
        for n, first, size in pack:
            out_ref[at : at + size] = refs[n][first : first + size, 0 : out_ref.shape[1]]
            at += size


def together(*blocks, packs=()):
    read = [n for _, pack in packs for n, first, size in pack]
    packed = [(sum(size for n, first, size in pack), columns) for columns, pack in packs]
    return pl.pallas_call(
        partial(hold_kernel, [pack for _, pack in packs]),
        in_specs=[
            pl.BlockSpec(memory_space=pltpu.VMEM if n in read else pl.ANY) for n in range(len(blocks))
        ],
        out_specs=[pl.BlockSpec(memory_space=pl.ANY)] * len(blocks)
        + [pl.BlockSpec(memory_space=pltpu.VMEM)] * len(packs),
        out_shape=[pltpu.VMEM(block.shape, block.dtype) for block in blocks]
        + [pltpu.VMEM(shape, jnp.bfloat16) for shape in packed],
        input_output_aliases={n: n for n in range(len(blocks))},
        compiler_params=pltpu.CompilerParams(vmem_limit_bytes=6 * 2**20),
        name="together",
    )(*in_vmem(blocks))


def copy_kernel(plan, facts, *refs):
    sem = refs[-1]
    group = facts[GROUP]
    copies = []
    for n, (source, out, row, column, flip, shape) in enumerate(plan):
        side = 1 - group if flip else group
        width = shape[-1]
        start = column[0] if flip is None else pl.multiple_of(side * width, width)
        view = refs[source].at[pl.ds(row[0], shape[0]), pl.ds(start, width)]
        target = refs[out].at[pl.ds(row[1], shape[0]), pl.ds(column[1], width)]
        copies.append(pltpu.make_async_copy(view, target, sem.at[n]))
    for copy in copies:
        copy.start()
    for copy in copies:
        copy.wait()


def take_parts(facts, sources, outs, plan):
    count = len(sources)
    plan = [(s, count + o, *rest) for s, o, *rest in plan]
    return pl.pallas_call(
        partial(copy_kernel, plan),
        grid_spec=pltpu.PrefetchScalarGridSpec(
            num_scalar_prefetch=1,
            grid=(),
            in_specs=[pl.BlockSpec(memory_space=pl.ANY)] * count,
            out_specs=[pl.BlockSpec(memory_space=pltpu.VMEM)] * len(outs),
            scratch_shapes=[pltpu.SemaphoreType.DMA((len(plan),))],
        ),
        out_shape=[pltpu.VMEM(shape, jnp.bfloat16) for shape in outs],
        compiler_params=pltpu.CompilerParams(vmem_limit_bytes=2**20),
        name="take_parts",
    )(facts, *in_hbm(sources))


def move(block, pairs):
    return lax.ppermute(block, "serve", pairs)


def across(block):
    return lax.ppermute(block, "groups", ACROSS)


GROUP, LENGTH, ORDER, TABLE = 0, 1, 2, 2 + CHIPS * CORES


def column_order(facts, slots, planes):
    rows, width = planes * 8, planes * HD
    row = lax.broadcasted_iota(jnp.int32, (rows, width), 0)
    col = lax.broadcasted_iota(jnp.int32, (rows, width), 1)
    place = (row // 8) * HD + row % 8
    parts = [(col == place + facts[ORDER + p] * 8).astype(jnp.float32) for p in range(slots)]
    return jnp.concatenate(parts, axis=0).astype(jnp.bfloat16)


def kv_kernel(facts, span_ref, req_ref, own_ref, sib_ref, *refs):
    slots = CHIPS * CORES
    pay_ref, new_ref, cache_ref, span_acc, req_acc = refs
    step = pl.program_id(0)
    chunk = span_ref.shape[2] // pl.num_programs(0)
    per_half = own_ref.shape[1] // chunk
    here = pl.ds(pl.multiple_of(step * chunk, chunk), chunk)
    columns = pl.ds(pl.multiple_of(step % per_half * chunk, chunk), chunk)
    size = own_ref.shape[0] // 2
    found = pl.ds(pl.multiple_of(step // per_half * size, size), size)
    w = jnp.concatenate([own_ref[found, columns], sib_ref[found, columns]], axis=0)
    x = jnp.concatenate([span_ref[0, :, here], req_ref[0, :, here]], axis=0)
    both = lax.dot_general(x, w, NT, preferred_element_type=jnp.float32)
    span_now, req_now = both[: span_ref.shape[1]], both[span_ref.shape[1] :]

    @pl.when(step == 0)
    def _():
        span_acc[...] = span_now
        req_acc[...] = req_now

    @pl.when(step > 0)
    def _():
        span_acc[...] += span_now
        req_acc[...] += req_now

    @pl.when(step == pl.num_programs(0) - 1)
    def _():
        order = column_order(facts, slots, 2)
        span_kv = jnp.dot(
            span_acc[...].astype(jnp.bfloat16), order, preferred_element_type=jnp.float32
        ).astype(jnp.bfloat16)
        new_ref[...] = jnp.dot(
            req_acc[...].astype(jnp.bfloat16), order, preferred_element_type=jnp.float32
        ).astype(jnp.bfloat16)
        tokens = span_kv.shape[0]
        pay_ref[0:tokens] = span_kv
        length = jnp.full((PAGE, 2 * HD), facts[LENGTH], jnp.int32)
        pay_ref[tokens:] = length.astype(jnp.float32).astype(jnp.bfloat16)
        for p in range(tokens // PAGE):
            cache_ref[facts[TABLE + p]] = span_kv[p * PAGE : (p + 1) * PAGE]


def project_kv(facts, span_states, recomp_states, blocks):
    tokens, width = span_states.shape[1:]
    rows = recomp_states.shape[1]
    steps = 4
    return pl.pallas_call(
        kv_kernel,
        grid_spec=pltpu.PrefetchScalarGridSpec(
            num_scalar_prefetch=1,
            grid=(steps,),
            in_specs=[
                *([pl.BlockSpec(memory_space=pltpu.VMEM)] * (2 + CORES)),
            ],
            out_specs=[
                pl.BlockSpec((tokens + PAGE, 2 * HD), lambda k, *_: (0, 0)),
                pl.BlockSpec((rows, 2 * HD), lambda k, *_: (0, 0)),
                pl.BlockSpec((tokens // PAGE, PAGE, 2 * HD), lambda k, *_: (0, 0, 0)),
            ],
            scratch_shapes=[
                pltpu.VMEM((tokens, 2 * HD), jnp.float32),
                pltpu.VMEM((rows, 2 * HD), jnp.float32),
            ],
        ),
        out_shape=[
            jax.ShapeDtypeStruct((tokens + PAGE, 2 * HD), jnp.bfloat16),
            jax.ShapeDtypeStruct((rows, 2 * HD), jnp.bfloat16),
            jax.ShapeDtypeStruct((tokens // PAGE, PAGE, 2 * HD), jnp.bfloat16),
        ],
        cost_estimate=pl.CostEstimate(flops=1000, bytes_accessed=1000, transcendentals=0),
        compiler_params=pltpu.CompilerParams(vmem_limit_bytes=16 * 2**20),
        name="project_kv",
    )(facts, span_states, recomp_states, *blocks)


def query_kernel(facts, mine_ref, own_ref, sib_ref, other_ref, *refs):
    mine_out, other_out, mine_acc, other_acc = refs
    step = pl.program_id(0)
    half = other_ref.shape[1]
    chunk = half // pl.num_programs(0)
    columns = pl.ds(pl.multiple_of(step * chunk, chunk), chunk)
    here = pl.ds(pl.multiple_of(facts[GROUP] * half + step * chunk, chunk), chunk)
    w = jnp.concatenate([own_ref[:, columns], sib_ref[:, columns]], axis=0)
    x = jnp.concatenate([mine_ref[0, :, here], other_ref[:, columns]], axis=0)
    both = lax.dot_general(x, w, NT, preferred_element_type=jnp.float32)
    mine_now, other_now = both[: mine_ref.shape[1]], both[mine_ref.shape[1] :]

    @pl.when(step == 0)
    def _():
        mine_acc[...] = mine_now
        other_acc[...] = other_now

    @pl.when(step > 0)
    def _():
        mine_acc[...] += mine_now
        other_acc[...] += other_now

    @pl.when(step == pl.num_programs(0) - 1)
    def _():
        mine_out[...] = mine_acc[...]
        other_out[...] = other_acc[...].astype(other_out.dtype)


def project_query(facts, recomp_states, other_rows, blocks, columns):
    rows = recomp_states.shape[1]
    depth = other_rows.shape[1]
    steps = 3
    return pl.pallas_call(
        query_kernel,
        grid_spec=pltpu.PrefetchScalarGridSpec(
            num_scalar_prefetch=1,
            grid=(steps,),
            in_specs=[
                *([pl.BlockSpec(memory_space=pltpu.VMEM)] * (CORES + 2)),
            ],
            out_specs=[
                pl.BlockSpec((rows, columns), lambda k, *_: (0, 0)),
                pl.BlockSpec((rows, columns), lambda k, *_: (0, 0)),
            ],
            scratch_shapes=[
                pltpu.VMEM((rows, columns), jnp.float32),
                pltpu.VMEM((rows, columns), jnp.float32),
            ],
        ),
        out_shape=[
            jax.ShapeDtypeStruct((rows, columns), jnp.float32),
            jax.ShapeDtypeStruct((rows, columns), jnp.bfloat16),
        ],
        cost_estimate=pl.CostEstimate(flops=1000, bytes_accessed=1000, transcendentals=0),
        compiler_params=pltpu.CompilerParams(vmem_limit_bytes=16 * 2**20),
        name="project_query",
    )(facts, recomp_states, *blocks, other_rows)


def attend_kernel(map_ref, facts, mine_ref, other_ref, new_ref, row_ref, *refs):
    out_ref, keys, values, lengths, bias = refs[CORES:]
    rows = new_ref.shape[0]
    cached = CPR * SPAN
    padded = keys.shape[0]
    sent = refs[0].shape[0] // CHIPS
    for s in range(CPR):
        slot = jnp.int32(0)
        for p in range(CHIPS * CORES):
            slot = jnp.where(facts[ORDER + p] == map_ref[s], p, slot)
        first = pl.multiple_of(slot % CHIPS * sent, 16)
        for c in range(CORES):

            @pl.when(slot // CHIPS == c)
            def _(s=s, first=first, ref=refs[c]):
                keys[s * SPAN : (s + 1) * SPAN] = ref[pl.ds(first, SPAN), 0:HD]
                values[s * SPAN : (s + 1) * SPAN] = ref[pl.ds(first, SPAN), HD : 2 * HD]
                lengths[s] = ref[pl.ds(first + SPAN, PAGE), :]
    keys[cached : cached + rows] = new_ref[:, 0:HD]
    values[cached : cached + rows] = new_ref[:, HD : 2 * HD]
    keys[cached + rows :] = jnp.zeros((padded - cached - rows, HD), jnp.bfloat16)
    values[cached + rows :] = jnp.zeros((padded - cached - rows, HD), jnp.bfloat16)
    new_pos = jnp.broadcast_to(row_ref[...], (rows, rows))
    diagonal = lax.broadcasted_iota(jnp.int32, (rows, rows), 0) == lax.broadcasted_iota(
        jnp.int32, (rows, rows), 1
    )
    mine_at = jnp.sum(jnp.where(diagonal, new_pos, 0), axis=1, keepdims=True)
    new_allowed = new_pos <= jnp.broadcast_to(mine_at, (rows, rows))
    mine_at = jnp.broadcast_to(mine_at, (rows, SPAN))
    lane = lax.broadcasted_iota(jnp.int32, (rows, SPAN), 1)
    blocked = jnp.float32(-jnp.inf)
    for s in range(CPR):
        key_pos = lane + s * SPAN
        redone = jnp.max(jnp.where(mine_at == key_pos, 1.0, 0.0), axis=0, keepdims=True)
        length = lengths[s].astype(jnp.float32)[0:1]
        offset = lax.broadcasted_iota(jnp.int32, (1, SPAN), 1).astype(jnp.float32)
        usable = jnp.where(offset < length, 1.0 - redone, 0.0)
        allowed = (jnp.broadcast_to(usable, (rows, SPAN)) > 0.5) & (key_pos <= mine_at)
        bias[:, s * SPAN : (s + 1) * SPAN] = jnp.where(allowed, 0.0, blocked)
    bias[:, cached:] = jnp.full((rows, padded - cached), blocked, jnp.float32)
    bias[:, cached : cached + rows] = jnp.where(new_allowed, 0.0, blocked)

    query = (mine_ref[...] + other_ref[...].astype(jnp.float32)).astype(jnp.bfloat16)
    heads = query.shape[1] // HD
    order = column_order(facts, CHIPS * CORES, heads)
    query = jnp.dot(query, order, preferred_element_type=jnp.float32).astype(jnp.bfloat16)
    for h in range(heads):
        scores = lax.dot_general(
            query[:, h * HD : (h + 1) * HD], keys[...], NT, preferred_element_type=jnp.float32
        )
        scores = scores * (HD ** (-0.5)) + bias[...]
        top = jnp.max(scores, axis=1, keepdims=True)
        weights = jnp.exp(scores - top)
        total = jnp.sum(weights, axis=1, keepdims=True)
        mixed = jnp.dot(weights.astype(jnp.bfloat16), values[...], preferred_element_type=jnp.float32)
        out_ref[:, h * HD : (h + 1) * HD] = (mixed / total).astype(jnp.bfloat16)


def attend(span_map, facts, mine, other, new_kv, positions, payloads):
    rows, columns = mine.shape
    cached = CPR * SPAN
    padded = cached + SPAN
    whole = lambda *shape: pl.BlockSpec(shape, lambda i, *_: (0,) * len(shape))
    return pl.pallas_call(
        attend_kernel,
        grid_spec=pltpu.PrefetchScalarGridSpec(
            num_scalar_prefetch=2,
            grid=(1,),
            in_specs=[
                whole(rows, columns),
                whole(rows, columns),
                whole(rows, 2 * HD),
                whole(1, rows),
                *([pl.BlockSpec(memory_space=pltpu.VMEM)] * CORES),
            ],
            out_specs=whole(rows, columns),
            scratch_shapes=[
                pltpu.VMEM((padded, HD), jnp.bfloat16),
                pltpu.VMEM((padded, HD), jnp.bfloat16),
                pltpu.VMEM((CPR, PAGE, 2 * HD), jnp.bfloat16),
                pltpu.VMEM((rows, padded), jnp.float32),
            ],
        ),
        out_shape=jax.ShapeDtypeStruct((rows, columns), jnp.bfloat16),
        cost_estimate=pl.CostEstimate(flops=1000, bytes_accessed=1000, transcendentals=0),
        compiler_params=pltpu.CompilerParams(vmem_limit_bytes=20 * 2**20),
        name="attend",
    )(span_map, facts, mine, other, new_kv, positions, *payloads)


def output_kernel(plan, arrived, facts, att_ref, att2_ref, *refs):
    out_ref, sent_ref, w_buf, o_buf, in_sem, out_sem, late_sem = refs[-7:]
    rows, columns = o_buf.shape[1:]
    share = columns // 6
    group = facts[GROUP]
    loads = []
    for p, (slot, parts) in enumerate(plan):
        copies = []
        for source, row, first, size in parts:
            ref = refs[source]
            if ref.shape[1] == columns:
                spans = [(0, 0, columns)]
            elif ref.shape[1] == share:
                spans = [(0, pl.multiple_of((1 - group) * share, share), share)]
            else:
                own = pl.multiple_of(group * share, share)
                spans = [(0, own, share), (share, 2 * share, columns - 2 * share)]
            for start, target, width in spans:
                view = ref.at[pl.ds(row, size), pl.ds(start, width)]
                goal = w_buf.at[p, pl.ds(first, size), pl.ds(target, width)]
                copy = pltpu.make_async_copy(view, goal, in_sem.at[p, len(copies)])
                copy.start()
                copies.append(copy)
        loads.append(copies)
    stores = place(facts, [(refs[source], slots) for source, slots in arrived], out_ref, late_sem)
    attended = jnp.concatenate([att_ref[...], att2_ref[...]], axis=0)
    width = columns // 3
    for p, (slot, parts) in enumerate(plan):
        for copy in loads[p]:
            copy.wait()
        for start in range(0, columns, width):
            both = jnp.dot(
                attended, w_buf[p, :, start : start + width], preferred_element_type=jnp.float32
            ).astype(jnp.bfloat16)
            o_buf[p, :, start : start + width] = both[:rows]
            sent_ref[p, :, start : start + width] = both[rows:]
        copy = pltpu.make_async_copy(
            o_buf.at[p], out_ref.at[0, :, columns_of(facts, slot, columns)], out_sem.at[p]
        )
        copy.start()
        stores.append(copy)
    for copy in stores:
        copy.wait()


def columns_of(facts, slot, columns):
    return pl.ds(pl.multiple_of(facts[ORDER + slot] * columns, columns), columns)


def place(facts, arrived, out_ref, sem):
    copies = []
    for ref, slots in arrived:
        for p, slot in enumerate(slots):
            target = out_ref.at[0, :, columns_of(facts, slot + CHIPS, ref.shape[2])]
            copy = pltpu.make_async_copy(ref.at[p], target, sem.at[len(copies)])
            copy.start()
            copies.append(copy)
    return copies


def place_kernel(slots, facts, *refs):
    before_ref, out_ref, sem = refs[-3:]
    for copy in place(facts, list(zip(refs, slots)), out_ref, sem):
        copy.wait()


def place_output(facts, arrived, before):
    blocks = [block for block, _ in arrived]
    slots = [slots for _, slots in arrived]
    return pl.pallas_call(
        partial(place_kernel, slots),
        grid_spec=pltpu.PrefetchScalarGridSpec(
            num_scalar_prefetch=1,
            grid=(),
            in_specs=[pl.BlockSpec(memory_space=pl.ANY)] * (len(blocks) + 1),
            out_specs=pl.BlockSpec(memory_space=pl.ANY),
            scratch_shapes=[pltpu.SemaphoreType.DMA((sum(map(len, slots)),))],
        ),
        out_shape=pltpu.HBM(before.shape, jnp.bfloat16),
        input_output_aliases={1 + len(blocks): 0},
        compiler_params=pltpu.CompilerParams(vmem_limit_bytes=2**20),
        name="place_output",
    )(facts, *blocks, *in_hbm([before]))


def project_output(facts, attended, before, work, arrived, width):
    rows, depth = attended[0].shape
    sources = []

    def index_of(block):
        if not any(block is held for held in sources):
            sources.append(block)
        return [block is held for held in sources].index(True)

    plan = [
        (slot, [(index_of(block), *where) for block, *where in parts]) for slot, parts in work
    ]
    arrived = [(index_of(block), slots) for block, slots in arrived]
    placed = sum(len(slots) for _, slots in arrived)
    columns = width // (CHIPS * CORES)
    filled = [] if before is None else [before]
    return pl.pallas_call(
        partial(output_kernel, plan, arrived),
        grid_spec=pltpu.PrefetchScalarGridSpec(
            num_scalar_prefetch=1,
            grid=(),
            in_specs=[pl.BlockSpec(memory_space=pltpu.VMEM)] * CORES
            + [pl.BlockSpec(memory_space=pl.ANY)] * (len(sources) + len(filled)),
            out_specs=[pl.BlockSpec(memory_space=pl.ANY), pl.BlockSpec(memory_space=pltpu.VMEM)],
            scratch_shapes=[
                pltpu.VMEM((len(plan), depth, columns), jnp.bfloat16),
                pltpu.VMEM((len(plan), rows, columns), jnp.bfloat16),
                pltpu.SemaphoreType.DMA((len(plan), 9)),
                pltpu.SemaphoreType.DMA((len(plan),)),
                pltpu.SemaphoreType.DMA((max(placed, 1),)),
            ],
        ),
        out_shape=[
            pltpu.HBM((1, rows, width), jnp.bfloat16),
            pltpu.VMEM((len(plan), rows, columns), jnp.bfloat16),
        ],
        input_output_aliases={1 + CORES + len(sources): 0} if filled else {},
        cost_estimate=pl.CostEstimate(flops=1000, bytes_accessed=1000, transcendentals=0),
        compiler_params=pltpu.CompilerParams(vmem_limit_bytes=(len(plan) * 3 + 6) * 2**20),
        name="project_output",
    )(facts, *attended, *sources, *in_hbm(filled))


def ring_body(
    span_states,
    recomp_states,
    w_query,
    w_kv,
    w_out,
    span_map,
    span_lengths,
    recompute_idx,
    block_table,
):
    pair = lambda ahead, back: (move(ahead, AHEAD), move(back, BACK))
    swap = lambda *blocks: tuple(move(block, SIBLING) for block in blocks)
    group = lax.axis_index("groups")
    width, heads, part = w_query.shape
    rows = recomp_states.shape[1]
    half = width // 2
    depth = heads * HD
    columns = w_out.shape[3]
    share = columns // 6
    order = jnp.asarray(slot_table())[lax.axis_index("serve")]
    facts = jnp.concatenate([group[None].astype(jnp.int32), span_lengths, order, block_table])

    query_rows = w_query.transpose(1, 2, 0).reshape(heads * part, width)
    kv_rows = w_kv.transpose(1, 2, 0).reshape(2 * part, width)
    own_out = w_out.reshape(depth, columns)
    cut = heads * part
    k0, q0 = take_parts(
        facts,
        [query_rows, kv_rows],
        [(4 * part, half), (cut, half)],
        [
            (1, 0, (0, 0), (0, 0), None, (2 * part, half)),
            (1, 0, (0, 2 * part), (half, 0), None, (2 * part, half)),
            (0, 1, (0, 0), (0, 0), False, (cut, half)),
        ],
    )
    cut = depth // 2
    theirs, top0, low0 = take_parts(
        facts,
        [recomp_states[0], own_out, k0],
        [(rows, half)] + [(cut, columns - share)] * 2,
        [(0, 0, (0, 0), (0, 0), True, (rows, half))]
        + [(1, 1 + n, (n * cut, 0), (0, 0), False, (cut, share)) for n in range(2)]
        + [
            (1, 1 + n, (n * cut, 0), (2 * share, share), None, (cut, columns - 2 * share))
            for n in range(2)
        ],
    )
    ka1, kb1 = together(*pair(k0, k0))
    qa1, qb1, ka1 = together(*pair(q0, q0), ka1)
    ka2, kb2, qa1 = together(*pair(ka1, kb1), qa1)
    qa2, qb2, ka2 = together(*pair(qa1, qb1), ka2)
    ka3, kb3, qa2 = together(*pair(ka2, kb2), qa2)
    qa3, qb3, ka3, top0 = together(*pair(qa2, qb2), ka3, top0)
    keys = (k0, ka1, kb1, ka2, kb2, ka3, kb3, move(kb3, BACK))
    queries = (q0, qa1, qb1, qa2, qb2, qa3, qb3, move(qa3, AHEAD))
    key_stack = (half, [(n, h * 2 * part, 2 * part) for h in range(2) for n in range(CHIPS)])
    query_stack = (half, [(CHIPS + n, 0, heads * part) for n in range(CHIPS)])
    *_, other_rows, low0, keys, queries = together(
        *keys, *queries, across(theirs), low0, packs=(key_stack, query_stack)
    )
    keys2, queries = lax.optimization_barrier((*swap(keys), queries))
    queries = (queries, *swap(queries))

    span0, new_kv, cache = project_kv(facts, span_states, recomp_states, (keys, keys2))
    ta1, tb1, span0 = together(*pair(top0, top0), span0)
    mine, theirs_part = project_query(facts, recomp_states, other_rows, queries, depth)
    sides = lambda *found: (share, [(n, 0, cut) for n in found])
    la1, lb1, sa1, sb1, theirs_part, ta1, tb1, send1 = together(
        *pair(low0, low0), *pair(span0, span0), theirs_part, ta1, tb1, packs=(sides(5, 0, 6, 1),)
    )
    ta2, tb2, sa2, sb2, other = together(*pair(ta1, tb1), *pair(sa1, sb1), across(theirs_part))
    la2, lb2, sa3, sb3, x1, ta2, tb2, send2 = together(
        *pair(la1, lb1), *pair(sa2, sb2), across(send1), ta2, tb2, packs=(sides(5, 0, 6, 1),)
    )
    spans = (span0, sa1, sb1, sa2, sb2, sa3, sb3, move(sa3, AHEAD))
    stack = (2 * HD, [(2 + n, 0, span0.shape[0]) for n in range(CHIPS)])
    quarter = lambda n, first: (columns - share, [(n, first, cut // 2)])
    ta3, tb3, *_, spans, top_ahead, top_back = together(
        *pair(ta2, tb2), *spans, packs=(stack, quarter(0, 0), quarter(1, cut // 2))
    )
    attended = attend(
        span_map[0], facts, mine, other, new_kv, recompute_idx, (spans, *swap(spans))
    )
    la3, lb3, x2, *attended = lax.optimization_barrier(
        (*pair(la2, lb2), across(send2), attended, *swap(attended))
    )
    la3, lb3, ta3, tb3, send3, low_ahead, low_back = together(
        la3,
        lb3,
        ta3,
        tb3,
        packs=(
            sides(2, 0, 3, 1),
            quarter(0, 0),
            quarter(1, cut // 2),
        ),
    )

    def near(slot, top, low, side, first):
        return slot, [(top, 0, 0, cut), (low, 0, cut, cut), (side, first * depth, 0, depth)]

    early = [
        (0, [(own_out, 0, 0, depth)]),
        near(1, ta1, la1, x1, 0),
        near(2, tb1, lb1, x1, 1),
        near(3, ta2, la2, x2, 0),
        near(4, tb2, lb2, x2, 1),
    ]
    width_out = CHIPS * CORES * columns
    result, sent1 = project_output(facts, attended, None, early, [], width_out)
    t4a, t4b, l4a, l4b, x3, sent1 = lax.optimization_barrier(
        (*pair(top_ahead, top_back), *pair(low_ahead, low_back), across(send3), sent1)
    )
    t4a, t4b, l4a, l4b, send4 = together(
        t4a, t4b, l4a, l4b, packs=((share, [(n, 0, cut // 2) for n in range(4)]),)
    )
    late = [near(5, ta3, la3, x3, 0), near(6, tb3, lb3, x3, 1)]
    result, sent2 = project_output(facts, attended, result, late, [], width_out)
    x4, arrived1, sent2 = lax.optimization_barrier((across(send4), *swap(sent1), sent2))
    arrived = [(arrived1, (0, 1, 2, 3, 4))]
    quarters = [(block, 0, n * cut // 2, cut // 2) for n, block in enumerate((t4a, t4b, l4a, l4b))]
    far = (7, [*quarters, (x4, 0, 0, depth)])
    result, sent3 = project_output(
        facts, attended, result, [far], arrived, width_out
    )
    arrived = [(swap(sent2)[0], (5, 6)), (swap(sent3)[0], (7,))]
    return (cache, place_output(facts, arrived, result))


def solution(mesh):
    in_specs = (
        P(("groups", "serve"), None, "tensor"),
        P(("groups", "serve"), None, "tensor"),
        P("tensor", None, "serve"),
        P("tensor", None, "serve"),
        P("tensor", None, None, "serve"),
        P(("groups", "serve"), None),
        P(("groups", "serve")),
        P(("groups", "serve"), None),
        P(("groups", "serve")),
    )
    out_specs = (P(("groups", "serve"), None, None), P(("groups", "serve"), None, "tensor"))
    body = ring_body if ring_fits(mesh) else general_body
    return jax.shard_map(body, mesh=mesh, in_specs=in_specs, out_specs=out_specs, check_vma=False)
```

```python
from functools import partial
import math

import jax
import jax.numpy as jnp
import numpy as np
from jax import lax
from jax.experimental import pallas as pl
from jax.experimental.pallas import tpu as pltpu
from jax.sharding import PartitionSpec as P

HD = 128
SPAN = 256
PAGE = 16
CPR = 6
PPC = 16


def merge_block(state, query, key_rows, value_rows, allowed, score_scale):
    old_max, old_sum, old_acc = state
    scores = (
        jnp.einsum("rhc,kc->rhk", query, key_rows, preferred_element_type=jnp.float32) * score_scale
    )
    block_max = jnp.max(jnp.where(allowed, scores, -jnp.inf), axis=2)
    new_max = jnp.maximum(old_max, block_max)
    weights_now = jnp.where(allowed, jnp.exp(scores - new_max[:, :, None]), 0.0)
    rescale = jnp.exp(old_max - new_max)
    new_acc = old_acc * rescale[:, :, None] + jnp.einsum(
        "rhk,kc->rhc", weights_now, value_rows.astype(jnp.float32)
    )
    return (new_max, old_sum * rescale + jnp.sum(weights_now, axis=2), new_acc)


def general_body(
    span_states,
    recomp_states,
    w_query,
    w_kv,
    w_out,
    span_map,
    span_lengths,
    recompute_idx,
    block_table,
):
    span_rows = span_states[0]
    req_rows = recomp_states[0]
    num_recomp = req_rows.shape[0]
    all_heads = w_query.shape[1]
    query_piece = lax.all_gather(w_query, "serve", axis=2, tiled=True)
    kv_piece = lax.all_gather(w_kv, "serve", axis=2, tiled=True)
    query_part = jnp.einsum(
        "rd,dhc->rhc", req_rows, query_piece, preferred_element_type=jnp.float32
    )
    new_part = jnp.einsum("rd,dhc->rhc", req_rows, kv_piece, preferred_element_type=jnp.float32)
    span_part = jnp.einsum("rd,dhc->rhc", span_rows, kv_piece, preferred_element_type=jnp.float32)
    query_full, new_full, span_full = lax.psum((query_part, new_part, span_part), "tensor")
    core_heads = all_heads // lax.axis_size("tensor")
    my_core = lax.axis_index("tensor")
    query = lax.dynamic_slice_in_dim(query_full, my_core * core_heads, core_heads, 1).astype(
        jnp.bfloat16
    )
    new_kv = new_full.astype(jnp.bfloat16)
    span_kv = span_full.astype(jnp.bfloat16)
    logical_pages = span_kv.reshape(PPC, PAGE, 2 * HD)
    inverse = jnp.argsort(block_table)
    physical = logical_pages[inverse]
    page_lens = jnp.repeat(span_lengths, PPC, total_repeat_length=PPC)
    positions = recompute_idx[0]
    my_spans = span_map[0]
    score_scale = HD ** (-0.5)
    slot_ids = jnp.arange(CPR, dtype=jnp.int32)
    token_ids = jnp.arange(PAGE, dtype=jnp.int32)
    local_allowed = (positions[None, :] <= positions[:, None])[:, None, :]
    empty_state = (
        jnp.full((num_recomp, core_heads), -jnp.inf, jnp.float32),
        jnp.zeros((num_recomp, core_heads), jnp.float32),
        jnp.zeros((num_recomp, core_heads, HD), jnp.float32),
    )
    state = merge_block(empty_state, query, new_kv[:, 0], new_kv[:, 1], local_allowed, score_scale)

    def block_update(skipping, totals, block):
        page_data, logical, lens_block, first_page = block
        width = page_data.shape[0]
        global_page = first_page + jnp.arange(width, dtype=jnp.int32)
        span_id = global_page // PPC
        matches = my_spans[None, :] == span_id[:, None]
        in_request = jnp.any(matches, axis=1)
        slot_num = jnp.sum(jnp.where(matches, slot_ids[None, :], 0), axis=1)
        offset = logical[:, None] * PAGE + token_ids[None, :]
        key_pos = (slot_num[:, None] * SPAN + offset).reshape(width * PAGE)
        usable = (in_request[:, None] & (offset < lens_block[:, None])).reshape(width * PAGE)
        redone = jnp.any(key_pos[:, None] == positions[None, :], axis=1)
        usable = usable & jnp.logical_not(redone)
        allowed = (usable[None, :] & (key_pos[None, :] <= positions[:, None]))[:, None, :]
        key_rows = page_data.reshape(width * PAGE, 2, HD)
        result = merge_block(totals, query, key_rows[:, 0], key_rows[:, 1], allowed, score_scale)
        return (result, None)

    page_data = lax.all_gather(physical, "serve", axis=0, tiled=True)
    logical = lax.all_gather(inverse, "serve", axis=0, tiled=True)
    lens_piece = lax.all_gather(page_lens, "serve", axis=0, tiled=True)
    count = page_data.shape[0]
    block = math.gcd(count, 64)
    steps_here = count // block
    blocks = (
        page_data.reshape(steps_here, block, PAGE, 2 * HD),
        logical.reshape(steps_here, block),
        lens_piece.reshape(steps_here, block),
        jnp.arange(steps_here, dtype=jnp.int32) * block,
    )
    result, unused_out = lax.scan(partial(block_update, False), state, blocks)
    state = result
    run_max, run_sum, run_acc = state
    attended = (run_acc / run_sum[:, :, None]).astype(jnp.bfloat16)
    partial_out = jnp.einsum(
        "rhc,hctd->rtd",
        attended,
        lax.all_gather(w_out, "serve", axis=3, tiled=True),
        preferred_element_type=jnp.float32,
    )
    reduced = lax.psum_scatter(
        partial_out.astype(jnp.bfloat16), "tensor", scatter_dimension=1, tiled=True
    )
    attn_out = reduced.reshape(1, reduced.shape[0], reduced.shape[2])
    return (physical, attn_out)


CHIPS = 8
CORES = 2
RING = ((0, 0), (1, 0), (2, 0), (3, 0), (3, 1), (2, 1), (1, 1), (0, 1))
CHIP_AT = tuple((z * 2 + y) * CORES for z, y in RING)
NT = (((1,), (1,)), ((), ()))


def ring_fits(mesh):
    return tuple(mesh.shape[name] for name in ("groups", "serve", "tensor")) == (2, CHIPS * CORES, 1)


def ring_pairs(step):
    return [
        (CHIP_AT[i] + c, CHIP_AT[(i + step) % CHIPS] + c) for i in range(CHIPS) for c in range(CORES)
    ]


AHEAD, BACK = ring_pairs(1), ring_pairs(-1)
SIBLING = [(i, i ^ 1) for i in range(CHIPS * CORES)]
ACROSS = [(0, 1), (1, 0)]


def slot_table():
    table = np.zeros((CHIPS * CORES, CHIPS * CORES), np.int32)
    for i in range(CHIPS):
        for c in range(CORES):
            for slot, step in enumerate((0, -1, 1, -2, 2, -3, 3, 4)):
                chip = CHIP_AT[(i + step) % CHIPS]
                table[CHIP_AT[i] + c, slot] = chip + c
                table[CHIP_AT[i] + c, CHIPS + slot] = chip + 1 - c
    return table


def in_hbm(blocks):
    return [pltpu.with_memory_space_constraint(block, pltpu.HBM) for block in blocks]


def in_vmem(blocks):
    return [pltpu.with_memory_space_constraint(block, pltpu.VMEM) for block in blocks]


def hold_kernel(packs, *refs):
    for pack, out_ref in zip(packs, refs[len(refs) - len(packs) :]):
        at = 0
        for n, first, size in pack:
            out_ref[at : at + size] = refs[n][first : first + size, 0 : out_ref.shape[1]]
            at += size


def together(*blocks, packs=()):
    read = [n for _, pack in packs for n, first, size in pack]
    packed = [(sum(size for n, first, size in pack), columns) for columns, pack in packs]
    return pl.pallas_call(
        partial(hold_kernel, [pack for _, pack in packs]),
        in_specs=[
            pl.BlockSpec(memory_space=pltpu.VMEM if n in read else pl.ANY) for n in range(len(blocks))
        ],
        out_specs=[pl.BlockSpec(memory_space=pl.ANY)] * len(blocks)
        + [pl.BlockSpec(memory_space=pltpu.VMEM)] * len(packs),
        out_shape=[pltpu.VMEM(block.shape, block.dtype) for block in blocks]
        + [pltpu.VMEM(shape, jnp.bfloat16) for shape in packed],
        input_output_aliases={n: n for n in range(len(blocks))},
        compiler_params=pltpu.CompilerParams(vmem_limit_bytes=6 * 2**20),
        name="together",
    )(*in_vmem(blocks))


def facts_kernel(group_ref, me_ref, len_ref, slot_ref, table_ref, out_ref):
    out_ref[GROUP] = group_ref[0]
    out_ref[LENGTH] = len_ref[0]
    for p in range(CHIPS * CORES):
        out_ref[ORDER + p] = slot_ref[me_ref[0] * CHIPS * CORES + p]
    for p in range(table_ref.shape[0]):
        out_ref[TABLE + p] = table_ref[p]


def list_facts(group, me, lengths, block_table):
    smem = pl.BlockSpec(memory_space=pltpu.SMEM)
    return pl.pallas_call(
        facts_kernel,
        in_specs=[smem] * 5,
        out_specs=smem,
        out_shape=jax.ShapeDtypeStruct((TABLE + block_table.shape[0],), jnp.int32),
        compiler_params=pltpu.CompilerParams(vmem_limit_bytes=2**20),
        name="list_facts",
    )(group, me, lengths, jnp.asarray(slot_table().reshape(-1)), block_table)


def copy_kernel(plan, count, group_ref, *refs):
    sem = refs[-1]
    refs = refs[count:]
    group = group_ref[0]
    copies = []
    for n, (source, out, row, column, flip, shape) in enumerate(plan):
        side = 1 - group if flip else group
        width = shape[-1]
        start = column[0] if flip is None else pl.multiple_of(side * width, width)
        view = refs[source].at[pl.ds(row[0], shape[0]), pl.ds(start, width)]
        target = refs[out].at[pl.ds(row[1], shape[0]), pl.ds(column[1], width)]
        copies.append(pltpu.make_async_copy(view, target, sem.at[n]))
    for copy in copies:
        copy.start()
    for copy in copies:
        copy.wait()


def take_parts(where, sources, outs, plan):
    count = len(sources)
    plan = [(s, count + o, *rest) for s, o, *rest in plan]
    return pl.pallas_call(
        partial(copy_kernel, plan, len(where) - 1),
        grid_spec=pltpu.PrefetchScalarGridSpec(
            num_scalar_prefetch=len(where),
            grid=(),
            in_specs=[pl.BlockSpec(memory_space=pl.ANY)] * count,
            out_specs=[pl.BlockSpec(memory_space=pltpu.VMEM)] * len(outs),
            scratch_shapes=[pltpu.SemaphoreType.DMA((len(plan),))],
        ),
        out_shape=[pltpu.VMEM(shape, jnp.bfloat16) for shape in outs],
        compiler_params=pltpu.CompilerParams(vmem_limit_bytes=2**20),
        name="take_parts",
    )(*where, *in_hbm(sources))


def move(block, pairs):
    return lax.ppermute(block, "serve", pairs)


def across(block):
    return lax.ppermute(block, "groups", ACROSS)


GROUP, LENGTH, ORDER, TABLE = 0, 1, 2, 2 + CHIPS * CORES


def column_order(facts, slots, planes):
    rows, width = planes * 8, planes * HD
    row = lax.broadcasted_iota(jnp.int32, (rows, width), 0)
    col = lax.broadcasted_iota(jnp.int32, (rows, width), 1)
    place = (row // 8) * HD + row % 8
    parts = [(col == place + facts[ORDER + p] * 8).astype(jnp.float32) for p in range(slots)]
    return jnp.concatenate(parts, axis=0).astype(jnp.bfloat16)


def kv_kernel(facts, span_ref, req_ref, own_ref, sib_ref, *refs):
    slots = CHIPS * CORES
    pay_ref, new_ref, cache_ref, span_acc, req_acc = refs
    step = pl.program_id(0)
    chunk = span_ref.shape[2] // pl.num_programs(0)
    per_half = own_ref.shape[1] // chunk
    here = pl.ds(pl.multiple_of(step * chunk, chunk), chunk)
    columns = pl.ds(pl.multiple_of(step % per_half * chunk, chunk), chunk)
    size = own_ref.shape[0] // 2
    found = pl.ds(pl.multiple_of(step // per_half * size, size), size)
    w = jnp.concatenate([own_ref[found, columns], sib_ref[found, columns]], axis=0)
    x = jnp.concatenate([span_ref[0, :, here], req_ref[0, :, here]], axis=0)
    both = lax.dot_general(x, w, NT, preferred_element_type=jnp.float32)
    span_now, req_now = both[: span_ref.shape[1]], both[span_ref.shape[1] :]

    @pl.when(step == 0)
    def _():
        span_acc[...] = span_now
        req_acc[...] = req_now

    @pl.when(step > 0)
    def _():
        span_acc[...] += span_now
        req_acc[...] += req_now

    @pl.when(step == pl.num_programs(0) - 1)
    def _():
        order = column_order(facts, slots, 2)
        span_kv = jnp.dot(
            span_acc[...].astype(jnp.bfloat16), order, preferred_element_type=jnp.float32
        ).astype(jnp.bfloat16)
        new_ref[...] = jnp.dot(
            req_acc[...].astype(jnp.bfloat16), order, preferred_element_type=jnp.float32
        ).astype(jnp.bfloat16)
        tokens = span_kv.shape[0]
        pay_ref[0:tokens] = span_kv
        length = jnp.full((PAGE, 2 * HD), facts[LENGTH], jnp.int32)
        pay_ref[tokens:] = length.astype(jnp.float32).astype(jnp.bfloat16)
        for p in range(tokens // PAGE):
            cache_ref[facts[TABLE + p]] = span_kv[p * PAGE : (p + 1) * PAGE]


def project_kv(facts, span_states, recomp_states, blocks):
    tokens, width = span_states.shape[1:]
    rows = recomp_states.shape[1]
    steps = 4
    return pl.pallas_call(
        kv_kernel,
        grid_spec=pltpu.PrefetchScalarGridSpec(
            num_scalar_prefetch=1,
            grid=(steps,),
            in_specs=[
                *([pl.BlockSpec(memory_space=pltpu.VMEM)] * (2 + CORES)),
            ],
            out_specs=[
                pl.BlockSpec((tokens + PAGE, 2 * HD), lambda k, *_: (0, 0)),
                pl.BlockSpec((rows, 2 * HD), lambda k, *_: (0, 0)),
                pl.BlockSpec((tokens // PAGE, PAGE, 2 * HD), lambda k, *_: (0, 0, 0)),
            ],
            scratch_shapes=[
                pltpu.VMEM((tokens, 2 * HD), jnp.float32),
                pltpu.VMEM((rows, 2 * HD), jnp.float32),
            ],
        ),
        out_shape=[
            jax.ShapeDtypeStruct((tokens + PAGE, 2 * HD), jnp.bfloat16),
            jax.ShapeDtypeStruct((rows, 2 * HD), jnp.bfloat16),
            jax.ShapeDtypeStruct((tokens // PAGE, PAGE, 2 * HD), jnp.bfloat16),
        ],
        cost_estimate=pl.CostEstimate(flops=1000, bytes_accessed=1000, transcendentals=0),
        compiler_params=pltpu.CompilerParams(vmem_limit_bytes=16 * 2**20),
        name="project_kv",
    )(facts, span_states, recomp_states, *blocks)


def query_kernel(facts, mine_ref, own_ref, sib_ref, other_ref, *refs):
    mine_out, other_out, mine_acc, other_acc = refs
    step = pl.program_id(0)
    half = other_ref.shape[1]
    chunk = half // pl.num_programs(0)
    columns = pl.ds(pl.multiple_of(step * chunk, chunk), chunk)
    here = pl.ds(pl.multiple_of(facts[GROUP] * half + step * chunk, chunk), chunk)
    w = jnp.concatenate([own_ref[:, columns], sib_ref[:, columns]], axis=0)
    x = jnp.concatenate([mine_ref[0, :, here], other_ref[:, columns]], axis=0)
    both = lax.dot_general(x, w, NT, preferred_element_type=jnp.float32)
    mine_now, other_now = both[: mine_ref.shape[1]], both[mine_ref.shape[1] :]

    @pl.when(step == 0)
    def _():
        mine_acc[...] = mine_now
        other_acc[...] = other_now

    @pl.when(step > 0)
    def _():
        mine_acc[...] += mine_now
        other_acc[...] += other_now

    @pl.when(step == pl.num_programs(0) - 1)
    def _():
        mine_out[...] = mine_acc[...]
        other_out[...] = other_acc[...].astype(other_out.dtype)


def project_query(facts, recomp_states, other_rows, blocks, columns):
    rows = recomp_states.shape[1]
    depth = other_rows.shape[1]
    steps = 3
    return pl.pallas_call(
        query_kernel,
        grid_spec=pltpu.PrefetchScalarGridSpec(
            num_scalar_prefetch=1,
            grid=(steps,),
            in_specs=[
                *([pl.BlockSpec(memory_space=pltpu.VMEM)] * (CORES + 2)),
            ],
            out_specs=[
                pl.BlockSpec((rows, columns), lambda k, *_: (0, 0)),
                pl.BlockSpec((rows, columns), lambda k, *_: (0, 0)),
            ],
            scratch_shapes=[
                pltpu.VMEM((rows, columns), jnp.float32),
                pltpu.VMEM((rows, columns), jnp.float32),
            ],
        ),
        out_shape=[
            jax.ShapeDtypeStruct((rows, columns), jnp.float32),
            jax.ShapeDtypeStruct((rows, columns), jnp.bfloat16),
        ],
        cost_estimate=pl.CostEstimate(flops=1000, bytes_accessed=1000, transcendentals=0),
        compiler_params=pltpu.CompilerParams(vmem_limit_bytes=16 * 2**20),
        name="project_query",
    )(facts, recomp_states, *blocks, other_rows)


def attend_kernel(map_ref, facts, mine_ref, other_ref, new_ref, row_ref, *refs):
    out_ref, keys, values, lengths, bias = refs[CORES:]
    rows = new_ref.shape[0]
    cached = CPR * SPAN
    padded = keys.shape[0]
    sent = refs[0].shape[0] // CHIPS
    for s in range(CPR):
        slot = jnp.int32(0)
        for p in range(CHIPS * CORES):
            slot = jnp.where(facts[ORDER + p] == map_ref[s], p, slot)
        first = pl.multiple_of(slot % CHIPS * sent, 16)
        for c in range(CORES):

            @pl.when(slot // CHIPS == c)
            def _(s=s, first=first, ref=refs[c]):
                keys[s * SPAN : (s + 1) * SPAN] = ref[pl.ds(first, SPAN), 0:HD]
                values[s * SPAN : (s + 1) * SPAN] = ref[pl.ds(first, SPAN), HD : 2 * HD]
                lengths[s] = ref[pl.ds(first + SPAN, PAGE), :]
    keys[cached : cached + rows] = new_ref[:, 0:HD]
    values[cached : cached + rows] = new_ref[:, HD : 2 * HD]
    keys[cached + rows :] = jnp.zeros((padded - cached - rows, HD), jnp.bfloat16)
    values[cached + rows :] = jnp.zeros((padded - cached - rows, HD), jnp.bfloat16)
    new_pos = jnp.broadcast_to(row_ref[...], (rows, rows))
    diagonal = lax.broadcasted_iota(jnp.int32, (rows, rows), 0) == lax.broadcasted_iota(
        jnp.int32, (rows, rows), 1
    )
    mine_at = jnp.sum(jnp.where(diagonal, new_pos, 0), axis=1, keepdims=True)
    new_allowed = new_pos <= jnp.broadcast_to(mine_at, (rows, rows))
    mine_at = jnp.broadcast_to(mine_at, (rows, SPAN))
    lane = lax.broadcasted_iota(jnp.int32, (rows, SPAN), 1)
    blocked = jnp.float32(-jnp.inf)
    for s in range(CPR):
        key_pos = lane + s * SPAN
        redone = jnp.max(jnp.where(mine_at == key_pos, 1.0, 0.0), axis=0, keepdims=True)
        length = lengths[s].astype(jnp.float32)[0:1]
        offset = lax.broadcasted_iota(jnp.int32, (1, SPAN), 1).astype(jnp.float32)
        usable = jnp.where(offset < length, 1.0 - redone, 0.0)
        allowed = (jnp.broadcast_to(usable, (rows, SPAN)) > 0.5) & (key_pos <= mine_at)
        bias[:, s * SPAN : (s + 1) * SPAN] = jnp.where(allowed, 0.0, blocked)
    bias[:, cached:] = jnp.full((rows, padded - cached), blocked, jnp.float32)
    bias[:, cached : cached + rows] = jnp.where(new_allowed, 0.0, blocked)

    query = (mine_ref[...] + other_ref[...].astype(jnp.float32)).astype(jnp.bfloat16)
    heads = query.shape[1] // HD
    order = column_order(facts, CHIPS * CORES, heads)
    query = jnp.dot(query, order, preferred_element_type=jnp.float32).astype(jnp.bfloat16)
    for h in range(heads):
        scores = lax.dot_general(
            query[:, h * HD : (h + 1) * HD], keys[...], NT, preferred_element_type=jnp.float32
        )
        scores = scores * (HD ** (-0.5)) + bias[...]
        top = jnp.max(scores, axis=1, keepdims=True)
        weights = jnp.exp(scores - top)
        total = jnp.sum(weights, axis=1, keepdims=True)
        mixed = jnp.dot(weights.astype(jnp.bfloat16), values[...], preferred_element_type=jnp.float32)
        out_ref[:, h * HD : (h + 1) * HD] = (mixed / total).astype(jnp.bfloat16)


def attend(span_map, facts, mine, other, new_kv, positions, payloads):
    rows, columns = mine.shape
    cached = CPR * SPAN
    padded = cached + SPAN
    whole = lambda *shape: pl.BlockSpec(shape, lambda i, *_: (0,) * len(shape))
    return pl.pallas_call(
        attend_kernel,
        grid_spec=pltpu.PrefetchScalarGridSpec(
            num_scalar_prefetch=2,
            grid=(1,),
            in_specs=[
                whole(rows, columns),
                whole(rows, columns),
                whole(rows, 2 * HD),
                whole(1, rows),
                *([pl.BlockSpec(memory_space=pltpu.VMEM)] * CORES),
            ],
            out_specs=whole(rows, columns),
            scratch_shapes=[
                pltpu.VMEM((padded, HD), jnp.bfloat16),
                pltpu.VMEM((padded, HD), jnp.bfloat16),
                pltpu.VMEM((CPR, PAGE, 2 * HD), jnp.bfloat16),
                pltpu.VMEM((rows, padded), jnp.float32),
            ],
        ),
        out_shape=jax.ShapeDtypeStruct((rows, columns), jnp.bfloat16),
        cost_estimate=pl.CostEstimate(flops=1000, bytes_accessed=1000, transcendentals=0),
        compiler_params=pltpu.CompilerParams(vmem_limit_bytes=20 * 2**20),
        name="attend",
    )(span_map, facts, mine, other, new_kv, positions, *payloads)


def output_kernel(plan, arrived, facts, att_ref, att2_ref, *refs):
    out_ref, sent_ref, w_buf, o_buf, in_sem, out_sem, late_sem = refs[-7:]
    rows, columns = o_buf.shape[1:]
    share = columns // 6
    group = facts[GROUP]
    loads = []
    for p, (slot, parts) in enumerate(plan):
        copies = []
        for source, row, first, size in parts:
            ref = refs[source]
            if ref.shape[1] == columns:
                spans = [(0, 0, columns)]
            elif ref.shape[1] == share:
                spans = [(0, pl.multiple_of((1 - group) * share, share), share)]
            else:
                own = pl.multiple_of(group * share, share)
                spans = [(0, own, share), (share, 2 * share, columns - 2 * share)]
            for start, target, width in spans:
                view = ref.at[pl.ds(row, size), pl.ds(start, width)]
                goal = w_buf.at[p, pl.ds(first, size), pl.ds(target, width)]
                copy = pltpu.make_async_copy(view, goal, in_sem.at[p, len(copies)])
                copy.start()
                copies.append(copy)
        loads.append(copies)
    stores = place(facts, [(refs[source], slots) for source, slots in arrived], out_ref, late_sem)
    attended = jnp.concatenate([att_ref[...], att2_ref[...]], axis=0)
    width = columns // 3
    for p, (slot, parts) in enumerate(plan):
        for copy in loads[p]:
            copy.wait()
        for start in range(0, columns, width):
            both = jnp.dot(
                attended, w_buf[p, :, start : start + width], preferred_element_type=jnp.float32
            ).astype(jnp.bfloat16)
            o_buf[p, :, start : start + width] = both[:rows]
            sent_ref[p, :, start : start + width] = both[rows:]
        copy = pltpu.make_async_copy(
            o_buf.at[p], out_ref.at[0, :, columns_of(facts, slot, columns)], out_sem.at[p]
        )
        copy.start()
        stores.append(copy)
    for copy in stores:
        copy.wait()


def columns_of(facts, slot, columns):
    return pl.ds(pl.multiple_of(facts[ORDER + slot] * columns, columns), columns)


def place(facts, arrived, out_ref, sem):
    copies = []
    for ref, slots in arrived:
        for p, slot in enumerate(slots):
            target = out_ref.at[0, :, columns_of(facts, slot + CHIPS, ref.shape[2])]
            copy = pltpu.make_async_copy(ref.at[p], target, sem.at[len(copies)])
            copy.start()
            copies.append(copy)
    return copies


def place_kernel(slots, facts, *refs):
    before_ref, out_ref, sem = refs[-3:]
    for copy in place(facts, list(zip(refs, slots)), out_ref, sem):
        copy.wait()


def place_output(facts, arrived, before):
    blocks = [block for block, _ in arrived]
    slots = [slots for _, slots in arrived]
    return pl.pallas_call(
        partial(place_kernel, slots),
        grid_spec=pltpu.PrefetchScalarGridSpec(
            num_scalar_prefetch=1,
            grid=(),
            in_specs=[pl.BlockSpec(memory_space=pl.ANY)] * (len(blocks) + 1),
            out_specs=pl.BlockSpec(memory_space=pl.ANY),
            scratch_shapes=[pltpu.SemaphoreType.DMA((sum(map(len, slots)),))],
        ),
        out_shape=pltpu.HBM(before.shape, jnp.bfloat16),
        input_output_aliases={1 + len(blocks): 0},
        compiler_params=pltpu.CompilerParams(vmem_limit_bytes=2**20),
        name="place_output",
    )(facts, *blocks, *in_hbm([before]))


def project_output(facts, attended, before, work, arrived, width):
    rows, depth = attended[0].shape
    sources = []

    def index_of(block):
        if not any(block is held for held in sources):
            sources.append(block)
        return [block is held for held in sources].index(True)

    plan = [
        (slot, [(index_of(block), *where) for block, *where in parts]) for slot, parts in work
    ]
    arrived = [(index_of(block), slots) for block, slots in arrived]
    placed = sum(len(slots) for _, slots in arrived)
    columns = width // (CHIPS * CORES)
    filled = [] if before is None else [before]
    return pl.pallas_call(
        partial(output_kernel, plan, arrived),
        grid_spec=pltpu.PrefetchScalarGridSpec(
            num_scalar_prefetch=1,
            grid=(),
            in_specs=[pl.BlockSpec(memory_space=pltpu.VMEM)] * CORES
            + [pl.BlockSpec(memory_space=pl.ANY)] * (len(sources) + len(filled)),
            out_specs=[pl.BlockSpec(memory_space=pl.ANY), pl.BlockSpec(memory_space=pltpu.VMEM)],
            scratch_shapes=[
                pltpu.VMEM((len(plan), depth, columns), jnp.bfloat16),
                pltpu.VMEM((len(plan), rows, columns), jnp.bfloat16),
                pltpu.SemaphoreType.DMA((len(plan), 10)),
                pltpu.SemaphoreType.DMA((len(plan),)),
                pltpu.SemaphoreType.DMA((max(placed, 1),)),
            ],
        ),
        out_shape=[
            pltpu.HBM((1, rows, width), jnp.bfloat16),
            pltpu.VMEM((len(plan), rows, columns), jnp.bfloat16),
        ],
        input_output_aliases={1 + CORES + len(sources): 0} if filled else {},
        cost_estimate=pl.CostEstimate(flops=1000, bytes_accessed=1000, transcendentals=0),
        compiler_params=pltpu.CompilerParams(vmem_limit_bytes=(len(plan) * 3 + 6) * 2**20),
        name="project_output",
    )(facts, *attended, *sources, *in_hbm(filled))


def ring_body(
    span_states,
    recomp_states,
    w_query,
    w_kv,
    w_out,
    span_map,
    span_lengths,
    recompute_idx,
    block_table,
):
    pair = lambda ahead, back: (move(ahead, AHEAD), move(back, BACK))
    swap = lambda *blocks: tuple(move(block, SIBLING) for block in blocks)
    group = lax.axis_index("groups")
    width, heads, part = w_query.shape
    rows = recomp_states.shape[1]
    half = width // 2
    depth = heads * HD
    columns = w_out.shape[3]
    share = columns // 6
    where = (group[None].astype(jnp.int32), lax.axis_index("serve")[None].astype(jnp.int32))

    query_rows = w_query.transpose(1, 2, 0).reshape(heads * part, width)
    kv_rows = w_kv.transpose(1, 2, 0).reshape(2 * part, width)
    own_out = w_out.reshape(depth, columns)
    cut = heads * part
    k0, q0 = take_parts(
        (*where, span_lengths),
        [query_rows, kv_rows],
        [(4 * part, half), (cut, half)],
        [
            (1, 0, (0, 0), (0, 0), None, (2 * part, half)),
            (1, 0, (0, 2 * part), (half, 0), None, (2 * part, half)),
            (0, 1, (0, 0), (0, 0), False, (cut, half)),
        ],
    )
    cut = depth // 2
    theirs, top0, low0 = take_parts(
        where,
        [recomp_states[0], own_out, k0],
        [(rows, half)] + [(cut, columns - share)] * 2,
        [(0, 0, (0, 0), (0, 0), True, (rows, half))]
        + [(1, 1 + n, (n * cut, 0), (0, 0), False, (cut, share)) for n in range(2)]
        + [
            (1, 1 + n, (n * cut, 0), (2 * share, share), None, (cut, columns - 2 * share))
            for n in range(2)
        ],
    )
    facts = list_facts(*where, span_lengths, block_table)
    ka1, kb1 = together(*pair(k0, k0))
    qa1, qb1, ka1 = together(*pair(q0, q0), ka1)
    ka2, kb2, qa1 = together(*pair(ka1, kb1), qa1)
    qa2, qb2, ka2 = together(*pair(qa1, qb1), ka2)
    ka3, kb3, qa2 = together(*pair(ka2, kb2), qa2)
    qa3, qb3, ka3, top0 = together(*pair(qa2, qb2), ka3, top0)
    keys = (k0, ka1, kb1, ka2, kb2, ka3, kb3, move(kb3, BACK))
    queries = (q0, qa1, qb1, qa2, qb2, qa3, qb3, move(qa3, AHEAD))
    key_stack = (half, [(n, h * 2 * part, 2 * part) for h in range(2) for n in range(CHIPS)])
    query_stack = (half, [(CHIPS + n, 0, heads * part) for n in range(CHIPS)])
    *_, other_rows, low0, keys, queries = together(
        *keys, *queries, across(theirs), low0, packs=(key_stack, query_stack)
    )
    keys = (keys, *swap(keys))

    span0, new_kv, cache = project_kv(facts, span_states, recomp_states, keys)
    sa1, sb1 = pair(span0, span0)
    sa2, sb2 = pair(sa1, sb1)
    sa3, sb3 = pair(sa2, sb2)
    ta1, tb1, queries = together(*pair(top0, top0), queries)
    mine, theirs_part = project_query(
        facts, recomp_states, other_rows, (queries, *swap(queries)), depth
    )
    sides = lambda *found: (share, [(n, 0, cut) for n in found])
    la1, lb1, ta1, tb1, send1 = together(
        *pair(low0, low0), ta1, tb1, packs=(sides(2, 0, 3, 1),)
    )
    ta2, tb2, la1 = together(*pair(ta1, tb1), la1)
    la2, lb2, x1, ta2, tb2, send2 = together(
        *pair(la1, lb1), across(send1), ta2, tb2, packs=(sides(3, 0, 4, 1),)
    )
    spans = (span0, sa1, sb1, sa2, sb2, sa3, sb3, move(sa3, AHEAD))
    stack = (2 * HD, [(n, 0, span0.shape[0]) for n in range(CHIPS)])
    *_, spans = together(*spans, packs=(stack,))
    other = across(theirs_part)
    attended = attend(
        span_map[0], facts, mine, other, new_kv, recompute_idx, (spans, *swap(spans))
    )
    attended = (attended, *swap(attended))
    quarter = lambda n, first: (columns - share, [(n, first, cut // 2)])
    ta3, tb3, top_ahead, top_back = together(
        *pair(ta2, tb2), packs=(quarter(0, 0), quarter(1, cut // 2))
    )
    la3, lb3, ta3, tb3, x2, send3, low_ahead, low_back = together(
        *pair(la2, lb2),
        ta3,
        tb3,
        across(send2),
        packs=(sides(2, 0, 3, 1), quarter(0, 0), quarter(1, cut // 2)),
    )

    def near(slot, top, low, side, first):
        return slot, [(top, 0, 0, cut), (low, 0, cut, cut), (side, first * depth, 0, depth)]

    early = [
        (0, [(own_out, 0, 0, depth)]),
        near(1, ta1, la1, x1, 0),
        near(2, tb1, lb1, x1, 1),
        near(3, ta2, la2, x2, 0),
        near(4, tb2, lb2, x2, 1),
    ]
    width_out = CHIPS * CORES * columns
    result, sent1 = project_output(facts, attended, None, early, [], width_out)
    t4a, t4b, l4a, l4b, x3, sent1 = lax.optimization_barrier(
        (*pair(top_ahead, top_back), *pair(low_ahead, low_back), across(send3), sent1)
    )
    x3, last_ahead, last_back = together(
        x3, packs=((share, [(0, 0, cut)]), (share, [(0, depth + cut, cut)]))
    )
    late = [near(5, ta3, la3, x3, 0), near(6, tb3, lb3, x3, 1)]
    result, sent2 = project_output(facts, attended, result, late, [], width_out)
    x4a, x4b, arrived1, sent2 = lax.optimization_barrier(
        (*pair(last_ahead, last_back), *swap(sent1), sent2)
    )
    arrived = [(arrived1, (0, 1, 2, 3, 4))]
    quarters = [(block, 0, n * cut // 2, cut // 2) for n, block in enumerate((t4a, t4b, l4a, l4b))]
    far = (7, [*quarters, (x4a, 0, 0, cut), (x4b, 0, cut, cut)])
    result, sent3 = project_output(
        facts, attended, result, [far], arrived, width_out
    )
    arrived = [(swap(sent2)[0], (5, 6)), (swap(sent3)[0], (7,))]
    return (cache, place_output(facts, arrived, result))


def solution(mesh):
    in_specs = (
        P(("groups", "serve"), None, "tensor"),
        P(("groups", "serve"), None, "tensor"),
        P("tensor", None, "serve"),
        P("tensor", None, "serve"),
        P("tensor", None, None, "serve"),
        P(("groups", "serve"), None),
        P(("groups", "serve")),
        P(("groups", "serve"), None),
        P(("groups", "serve")),
    )
    out_specs = (P(("groups", "serve"), None, None), P(("groups", "serve"), None, "tensor"))
    body = ring_body if ring_fits(mesh) else general_body
    return jax.shard_map(body, mesh=mesh, in_specs=in_specs, out_specs=out_specs, check_vma=False)
```

```python
from functools import partial
import math

import jax
import jax.numpy as jnp
import numpy as np
from jax import lax
from jax.experimental import pallas as pl
from jax.experimental.pallas import tpu as pltpu
from jax.sharding import PartitionSpec as P

HD = 128
SPAN = 256
PAGE = 16
CPR = 6
PPC = 16


def merge_block(state, query, key_rows, value_rows, allowed, score_scale):
    old_max, old_sum, old_acc = state
    scores = (
        jnp.einsum("rhc,kc->rhk", query, key_rows, preferred_element_type=jnp.float32) * score_scale
    )
    block_max = jnp.max(jnp.where(allowed, scores, -jnp.inf), axis=2)
    new_max = jnp.maximum(old_max, block_max)
    weights_now = jnp.where(allowed, jnp.exp(scores - new_max[:, :, None]), 0.0)
    rescale = jnp.exp(old_max - new_max)
    new_acc = old_acc * rescale[:, :, None] + jnp.einsum(
        "rhk,kc->rhc", weights_now, value_rows.astype(jnp.float32)
    )
    return (new_max, old_sum * rescale + jnp.sum(weights_now, axis=2), new_acc)


def general_body(
    span_states,
    recomp_states,
    w_query,
    w_kv,
    w_out,
    span_map,
    span_lengths,
    recompute_idx,
    block_table,
):
    span_rows = span_states[0]
    req_rows = recomp_states[0]
    num_recomp = req_rows.shape[0]
    all_heads = w_query.shape[1]
    query_piece = lax.all_gather(w_query, "serve", axis=2, tiled=True)
    kv_piece = lax.all_gather(w_kv, "serve", axis=2, tiled=True)
    query_part = jnp.einsum(
        "rd,dhc->rhc", req_rows, query_piece, preferred_element_type=jnp.float32
    )
    new_part = jnp.einsum("rd,dhc->rhc", req_rows, kv_piece, preferred_element_type=jnp.float32)
    span_part = jnp.einsum("rd,dhc->rhc", span_rows, kv_piece, preferred_element_type=jnp.float32)
    query_full, new_full, span_full = lax.psum((query_part, new_part, span_part), "tensor")
    core_heads = all_heads // lax.axis_size("tensor")
    my_core = lax.axis_index("tensor")
    query = lax.dynamic_slice_in_dim(query_full, my_core * core_heads, core_heads, 1).astype(
        jnp.bfloat16
    )
    new_kv = new_full.astype(jnp.bfloat16)
    span_kv = span_full.astype(jnp.bfloat16)
    logical_pages = span_kv.reshape(PPC, PAGE, 2 * HD)
    inverse = jnp.argsort(block_table)
    physical = logical_pages[inverse]
    page_lens = jnp.repeat(span_lengths, PPC, total_repeat_length=PPC)
    positions = recompute_idx[0]
    my_spans = span_map[0]
    score_scale = HD ** (-0.5)
    slot_ids = jnp.arange(CPR, dtype=jnp.int32)
    token_ids = jnp.arange(PAGE, dtype=jnp.int32)
    local_allowed = (positions[None, :] <= positions[:, None])[:, None, :]
    empty_state = (
        jnp.full((num_recomp, core_heads), -jnp.inf, jnp.float32),
        jnp.zeros((num_recomp, core_heads), jnp.float32),
        jnp.zeros((num_recomp, core_heads, HD), jnp.float32),
    )
    state = merge_block(empty_state, query, new_kv[:, 0], new_kv[:, 1], local_allowed, score_scale)

    def block_update(skipping, totals, block):
        page_data, logical, lens_block, first_page = block
        width = page_data.shape[0]
        global_page = first_page + jnp.arange(width, dtype=jnp.int32)
        span_id = global_page // PPC
        matches = my_spans[None, :] == span_id[:, None]
        in_request = jnp.any(matches, axis=1)
        slot_num = jnp.sum(jnp.where(matches, slot_ids[None, :], 0), axis=1)
        offset = logical[:, None] * PAGE + token_ids[None, :]
        key_pos = (slot_num[:, None] * SPAN + offset).reshape(width * PAGE)
        usable = (in_request[:, None] & (offset < lens_block[:, None])).reshape(width * PAGE)
        redone = jnp.any(key_pos[:, None] == positions[None, :], axis=1)
        usable = usable & jnp.logical_not(redone)
        allowed = (usable[None, :] & (key_pos[None, :] <= positions[:, None]))[:, None, :]
        key_rows = page_data.reshape(width * PAGE, 2, HD)
        result = merge_block(totals, query, key_rows[:, 0], key_rows[:, 1], allowed, score_scale)
        return (result, None)

    page_data = lax.all_gather(physical, "serve", axis=0, tiled=True)
    logical = lax.all_gather(inverse, "serve", axis=0, tiled=True)
    lens_piece = lax.all_gather(page_lens, "serve", axis=0, tiled=True)
    count = page_data.shape[0]
    block = math.gcd(count, 64)
    steps_here = count // block
    blocks = (
        page_data.reshape(steps_here, block, PAGE, 2 * HD),
        logical.reshape(steps_here, block),
        lens_piece.reshape(steps_here, block),
        jnp.arange(steps_here, dtype=jnp.int32) * block,
    )
    result, unused_out = lax.scan(partial(block_update, False), state, blocks)
    state = result
    run_max, run_sum, run_acc = state
    attended = (run_acc / run_sum[:, :, None]).astype(jnp.bfloat16)
    partial_out = jnp.einsum(
        "rhc,hctd->rtd",
        attended,
        lax.all_gather(w_out, "serve", axis=3, tiled=True),
        preferred_element_type=jnp.float32,
    )
    reduced = lax.psum_scatter(
        partial_out.astype(jnp.bfloat16), "tensor", scatter_dimension=1, tiled=True
    )
    attn_out = reduced.reshape(1, reduced.shape[0], reduced.shape[2])
    return (physical, attn_out)


CHIPS = 8
CORES = 2
RING = ((0, 0), (1, 0), (2, 0), (3, 0), (3, 1), (2, 1), (1, 1), (0, 1))
CHIP_AT = tuple((z * 2 + y) * CORES for z, y in RING)
NT = (((1,), (1,)), ((), ()))


def ring_fits(mesh):
    return tuple(mesh.shape[name] for name in ("groups", "serve", "tensor")) == (2, CHIPS * CORES, 1)


def ring_pairs(step):
    return [
        (CHIP_AT[i] + c, CHIP_AT[(i + step) % CHIPS] + c) for i in range(CHIPS) for c in range(CORES)
    ]


AHEAD, BACK = ring_pairs(1), ring_pairs(-1)
SIBLING = [(i, i ^ 1) for i in range(CHIPS * CORES)]
ACROSS = [(0, 1), (1, 0)]


def slot_table():
    table = np.zeros((CHIPS * CORES, CHIPS * CORES), np.int32)
    for i in range(CHIPS):
        for c in range(CORES):
            for slot, step in enumerate((0, -1, 1, -2, 2, -3, 3, 4)):
                chip = CHIP_AT[(i + step) % CHIPS]
                table[CHIP_AT[i] + c, slot] = chip + c
                table[CHIP_AT[i] + c, CHIPS + slot] = chip + 1 - c
    return table


def in_hbm(blocks):
    return [pltpu.with_memory_space_constraint(block, pltpu.HBM) for block in blocks]


def in_vmem(blocks):
    return [pltpu.with_memory_space_constraint(block, pltpu.VMEM) for block in blocks]


def hold_kernel(packs, *refs):
    for pack, out_ref in zip(packs, refs[len(refs) - len(packs) :]):
        at = 0
        for n, first, size in pack:
            out_ref[at : at + size] = refs[n][first : first + size, 0 : out_ref.shape[1]]
            at += size


def together(*blocks, packs=()):
    read = [n for _, pack in packs for n, first, size in pack]
    packed = [(sum(size for n, first, size in pack), columns) for columns, pack in packs]
    return pl.pallas_call(
        partial(hold_kernel, [pack for _, pack in packs]),
        in_specs=[
            pl.BlockSpec(memory_space=pltpu.VMEM if n in read else pl.ANY) for n in range(len(blocks))
        ],
        out_specs=[pl.BlockSpec(memory_space=pl.ANY)] * len(blocks)
        + [pl.BlockSpec(memory_space=pltpu.VMEM)] * len(packs),
        out_shape=[pltpu.VMEM(block.shape, block.dtype) for block in blocks]
        + [pltpu.VMEM(shape, jnp.bfloat16) for shape in packed],
        input_output_aliases={n: n for n in range(len(blocks))},
        compiler_params=pltpu.CompilerParams(vmem_limit_bytes=6 * 2**20),
        name="together",
    )(*in_vmem(blocks))


def facts_kernel(group_ref, me_ref, len_ref, slot_ref, table_ref, out_ref):
    out_ref[GROUP] = group_ref[0]
    out_ref[LENGTH] = len_ref[0]
    for p in range(CHIPS * CORES):
        out_ref[ORDER + p] = slot_ref[me_ref[0] * CHIPS * CORES + p]
    for p in range(table_ref.shape[0]):
        out_ref[TABLE + p] = table_ref[p]


def list_facts(group, me, lengths, block_table):
    smem = pl.BlockSpec(memory_space=pltpu.SMEM)
    return pl.pallas_call(
        facts_kernel,
        in_specs=[smem] * 5,
        out_specs=smem,
        out_shape=jax.ShapeDtypeStruct((TABLE + block_table.shape[0],), jnp.int32),
        compiler_params=pltpu.CompilerParams(vmem_limit_bytes=2**20),
        name="list_facts",
    )(group, me, lengths, jnp.asarray(slot_table().reshape(-1)), block_table)


def copy_kernel(plan, count, group_ref, *refs):
    sem = refs[-1]
    refs = refs[count:]
    group = group_ref[0]
    copies = []
    for n, (source, out, row, column, flip, shape) in enumerate(plan):
        side = 1 - group if flip else group
        width = shape[-1]
        start = column[0] if flip is None else pl.multiple_of(side * width, width)
        view = refs[source].at[pl.ds(row[0], shape[0]), pl.ds(start, width)]
        target = refs[out].at[pl.ds(row[1], shape[0]), pl.ds(column[1], width)]
        copies.append(pltpu.make_async_copy(view, target, sem.at[n]))
    for copy in copies:
        copy.start()
    for copy in copies:
        copy.wait()


def take_parts(where, sources, outs, plan):
    count = len(sources)
    plan = [(s, count + o, *rest) for s, o, *rest in plan]
    return pl.pallas_call(
        partial(copy_kernel, plan, len(where) - 1),
        grid_spec=pltpu.PrefetchScalarGridSpec(
            num_scalar_prefetch=len(where),
            grid=(),
            in_specs=[pl.BlockSpec(memory_space=pl.ANY)] * count,
            out_specs=[pl.BlockSpec(memory_space=pltpu.VMEM)] * len(outs),
            scratch_shapes=[pltpu.SemaphoreType.DMA((len(plan),))],
        ),
        out_shape=[pltpu.VMEM(shape, jnp.bfloat16) for shape in outs],
        compiler_params=pltpu.CompilerParams(vmem_limit_bytes=2**20),
        name="take_parts",
    )(*where, *in_hbm(sources))


def move(block, pairs):
    return lax.ppermute(block, "serve", pairs)


def across(block):
    return lax.ppermute(block, "groups", ACROSS)


GROUP, LENGTH, ORDER, TABLE = 0, 1, 2, 2 + CHIPS * CORES


def column_order(facts, slots, planes):
    rows, width = planes * 8, planes * HD
    row = lax.broadcasted_iota(jnp.int32, (rows, width), 0)
    col = lax.broadcasted_iota(jnp.int32, (rows, width), 1)
    place = (row // 8) * HD + row % 8
    parts = [(col == place + facts[ORDER + p] * 8).astype(jnp.float32) for p in range(slots)]
    return jnp.concatenate(parts, axis=0).astype(jnp.bfloat16)


def kv_kernel(facts, span_ref, req_ref, own_ref, sib_ref, *refs):
    slots = CHIPS * CORES
    pay_ref, new_ref, cache_ref, span_acc, req_acc = refs
    step = pl.program_id(0)
    chunk = span_ref.shape[2] // pl.num_programs(0)
    per_half = own_ref.shape[1] // chunk
    here = pl.ds(pl.multiple_of(step * chunk, chunk), chunk)
    columns = pl.ds(pl.multiple_of(step % per_half * chunk, chunk), chunk)
    size = own_ref.shape[0] // 2
    found = pl.ds(pl.multiple_of(step // per_half * size, size), size)
    w = jnp.concatenate([own_ref[found, columns], sib_ref[found, columns]], axis=0)
    x = jnp.concatenate([span_ref[0, :, here], req_ref[0, :, here]], axis=0)
    both = lax.dot_general(x, w, NT, preferred_element_type=jnp.float32)
    span_now, req_now = both[: span_ref.shape[1]], both[span_ref.shape[1] :]

    @pl.when(step == 0)
    def _():
        span_acc[...] = span_now
        req_acc[...] = req_now

    @pl.when(step > 0)
    def _():
        span_acc[...] += span_now
        req_acc[...] += req_now

    @pl.when(step == pl.num_programs(0) - 1)
    def _():
        order = column_order(facts, slots, 2)
        span_kv = jnp.dot(
            span_acc[...].astype(jnp.bfloat16), order, preferred_element_type=jnp.float32
        ).astype(jnp.bfloat16)
        new_ref[...] = jnp.dot(
            req_acc[...].astype(jnp.bfloat16), order, preferred_element_type=jnp.float32
        ).astype(jnp.bfloat16)
        tokens = span_kv.shape[0]
        pay_ref[0:tokens] = span_kv
        length = jnp.full((PAGE, 2 * HD), facts[LENGTH], jnp.int32)
        pay_ref[tokens:] = length.astype(jnp.float32).astype(jnp.bfloat16)
        for p in range(tokens // PAGE):
            cache_ref[facts[TABLE + p]] = span_kv[p * PAGE : (p + 1) * PAGE]


def project_kv(facts, span_states, recomp_states, blocks):
    tokens, width = span_states.shape[1:]
    rows = recomp_states.shape[1]
    steps = 4
    return pl.pallas_call(
        kv_kernel,
        grid_spec=pltpu.PrefetchScalarGridSpec(
            num_scalar_prefetch=1,
            grid=(steps,),
            in_specs=[
                *([pl.BlockSpec(memory_space=pltpu.VMEM)] * (2 + CORES)),
            ],
            out_specs=[
                pl.BlockSpec((tokens + PAGE, 2 * HD), lambda k, *_: (0, 0)),
                pl.BlockSpec((rows, 2 * HD), lambda k, *_: (0, 0)),
                pl.BlockSpec((tokens // PAGE, PAGE, 2 * HD), lambda k, *_: (0, 0, 0)),
            ],
            scratch_shapes=[
                pltpu.VMEM((tokens, 2 * HD), jnp.float32),
                pltpu.VMEM((rows, 2 * HD), jnp.float32),
            ],
        ),
        out_shape=[
            jax.ShapeDtypeStruct((tokens + PAGE, 2 * HD), jnp.bfloat16),
            jax.ShapeDtypeStruct((rows, 2 * HD), jnp.bfloat16),
            jax.ShapeDtypeStruct((tokens // PAGE, PAGE, 2 * HD), jnp.bfloat16),
        ],
        cost_estimate=pl.CostEstimate(flops=1000, bytes_accessed=1000, transcendentals=0),
        compiler_params=pltpu.CompilerParams(vmem_limit_bytes=16 * 2**20),
        name="project_kv",
    )(facts, span_states, recomp_states, *blocks)


def query_kernel(facts, mine_ref, own_ref, sib_ref, other_ref, *refs):
    mine_out, other_out, mine_acc, other_acc = refs
    step = pl.program_id(0)
    half = other_ref.shape[1]
    chunk = half // pl.num_programs(0)
    columns = pl.ds(pl.multiple_of(step * chunk, chunk), chunk)
    here = pl.ds(pl.multiple_of(facts[GROUP] * half + step * chunk, chunk), chunk)
    w = jnp.concatenate([own_ref[:, columns], sib_ref[:, columns]], axis=0)
    x = jnp.concatenate([mine_ref[0, :, here], other_ref[:, columns]], axis=0)
    both = lax.dot_general(x, w, NT, preferred_element_type=jnp.float32)
    mine_now, other_now = both[: mine_ref.shape[1]], both[mine_ref.shape[1] :]

    @pl.when(step == 0)
    def _():
        mine_acc[...] = mine_now
        other_acc[...] = other_now

    @pl.when(step > 0)
    def _():
        mine_acc[...] += mine_now
        other_acc[...] += other_now

    @pl.when(step == pl.num_programs(0) - 1)
    def _():
        mine_out[...] = mine_acc[...]
        other_out[...] = other_acc[...].astype(other_out.dtype)


def project_query(facts, recomp_states, other_rows, blocks, columns):
    rows = recomp_states.shape[1]
    depth = other_rows.shape[1]
    steps = 3
    return pl.pallas_call(
        query_kernel,
        grid_spec=pltpu.PrefetchScalarGridSpec(
            num_scalar_prefetch=1,
            grid=(steps,),
            in_specs=[
                *([pl.BlockSpec(memory_space=pltpu.VMEM)] * (CORES + 2)),
            ],
            out_specs=[
                pl.BlockSpec((rows, columns), lambda k, *_: (0, 0)),
                pl.BlockSpec((rows, columns), lambda k, *_: (0, 0)),
            ],
            scratch_shapes=[
                pltpu.VMEM((rows, columns), jnp.float32),
                pltpu.VMEM((rows, columns), jnp.float32),
            ],
        ),
        out_shape=[
            jax.ShapeDtypeStruct((rows, columns), jnp.float32),
            jax.ShapeDtypeStruct((rows, columns), jnp.bfloat16),
        ],
        cost_estimate=pl.CostEstimate(flops=1000, bytes_accessed=1000, transcendentals=0),
        compiler_params=pltpu.CompilerParams(vmem_limit_bytes=16 * 2**20),
        name="project_query",
    )(facts, recomp_states, *blocks, other_rows)


def attend_kernel(map_ref, facts, mine_ref, other_ref, new_ref, row_ref, *refs):
    out_ref, keys, values, lengths, bias = refs[CORES:]
    rows = new_ref.shape[0]
    cached = CPR * SPAN
    padded = keys.shape[0]
    sent = refs[0].shape[0] // CHIPS
    for s in range(CPR):
        slot = jnp.int32(0)
        for p in range(CHIPS * CORES):
            slot = jnp.where(facts[ORDER + p] == map_ref[s], p, slot)
        first = pl.multiple_of(slot % CHIPS * sent, 16)
        for c in range(CORES):

            @pl.when(slot // CHIPS == c)
            def _(s=s, first=first, ref=refs[c]):
                keys[s * SPAN : (s + 1) * SPAN] = ref[pl.ds(first, SPAN), 0:HD]
                values[s * SPAN : (s + 1) * SPAN] = ref[pl.ds(first, SPAN), HD : 2 * HD]
                lengths[s] = ref[pl.ds(first + SPAN, PAGE), :]
    keys[cached : cached + rows] = new_ref[:, 0:HD]
    values[cached : cached + rows] = new_ref[:, HD : 2 * HD]
    keys[cached + rows :] = jnp.zeros((padded - cached - rows, HD), jnp.bfloat16)
    values[cached + rows :] = jnp.zeros((padded - cached - rows, HD), jnp.bfloat16)
    new_pos = jnp.broadcast_to(row_ref[...], (rows, rows))
    diagonal = lax.broadcasted_iota(jnp.int32, (rows, rows), 0) == lax.broadcasted_iota(
        jnp.int32, (rows, rows), 1
    )
    mine_at = jnp.sum(jnp.where(diagonal, new_pos, 0), axis=1, keepdims=True)
    new_allowed = new_pos <= jnp.broadcast_to(mine_at, (rows, rows))
    mine_at = jnp.broadcast_to(mine_at, (rows, SPAN))
    lane = lax.broadcasted_iota(jnp.int32, (rows, SPAN), 1)
    blocked = jnp.float32(-jnp.inf)
    for s in range(CPR):
        key_pos = lane + s * SPAN
        redone = jnp.max(jnp.where(mine_at == key_pos, 1.0, 0.0), axis=0, keepdims=True)
        length = lengths[s].astype(jnp.float32)[0:1]
        offset = lax.broadcasted_iota(jnp.int32, (1, SPAN), 1).astype(jnp.float32)
        usable = jnp.where(offset < length, 1.0 - redone, 0.0)
        allowed = (jnp.broadcast_to(usable, (rows, SPAN)) > 0.5) & (key_pos <= mine_at)
        bias[:, s * SPAN : (s + 1) * SPAN] = jnp.where(allowed, 0.0, blocked)
    bias[:, cached:] = jnp.full((rows, padded - cached), blocked, jnp.float32)
    bias[:, cached : cached + rows] = jnp.where(new_allowed, 0.0, blocked)

    query = (mine_ref[...] + other_ref[...].astype(jnp.float32)).astype(jnp.bfloat16)
    heads = query.shape[1] // HD
    order = column_order(facts, CHIPS * CORES, heads)
    query = jnp.dot(query, order, preferred_element_type=jnp.float32).astype(jnp.bfloat16)
    for h in range(heads):
        scores = lax.dot_general(
            query[:, h * HD : (h + 1) * HD], keys[...], NT, preferred_element_type=jnp.float32
        )
        scores = scores * (HD ** (-0.5)) + bias[...]
        top = jnp.max(scores, axis=1, keepdims=True)
        weights = jnp.exp(scores - top)
        total = jnp.sum(weights, axis=1, keepdims=True)
        mixed = jnp.dot(weights.astype(jnp.bfloat16), values[...], preferred_element_type=jnp.float32)
        out_ref[:, h * HD : (h + 1) * HD] = (mixed / total).astype(jnp.bfloat16)


def attend(span_map, facts, mine, other, new_kv, positions, payloads):
    rows, columns = mine.shape
    cached = CPR * SPAN
    padded = cached + SPAN
    whole = lambda *shape: pl.BlockSpec(shape, lambda i, *_: (0,) * len(shape))
    return pl.pallas_call(
        attend_kernel,
        grid_spec=pltpu.PrefetchScalarGridSpec(
            num_scalar_prefetch=2,
            grid=(1,),
            in_specs=[
                whole(rows, columns),
                whole(rows, columns),
                whole(rows, 2 * HD),
                whole(1, rows),
                *([pl.BlockSpec(memory_space=pltpu.VMEM)] * CORES),
            ],
            out_specs=whole(rows, columns),
            scratch_shapes=[
                pltpu.VMEM((padded, HD), jnp.bfloat16),
                pltpu.VMEM((padded, HD), jnp.bfloat16),
                pltpu.VMEM((CPR, PAGE, 2 * HD), jnp.bfloat16),
                pltpu.VMEM((rows, padded), jnp.float32),
            ],
        ),
        out_shape=jax.ShapeDtypeStruct((rows, columns), jnp.bfloat16),
        cost_estimate=pl.CostEstimate(flops=1000, bytes_accessed=1000, transcendentals=0),
        compiler_params=pltpu.CompilerParams(vmem_limit_bytes=20 * 2**20),
        name="attend",
    )(span_map, facts, mine, other, new_kv, positions, *payloads)


def output_kernel(plan, arrived, facts, att_ref, att2_ref, *refs):
    out_ref, sent_ref, o_buf, out_sem, late_sem = refs[-5:]
    rows, columns = o_buf.shape[1:]
    share = columns // 6
    wide = 2 * share
    group = facts[GROUP]
    stores = place(facts, [(refs[source], slots) for source, slots in arrived], out_ref, late_sem)
    attended = jnp.concatenate([att_ref[...], att2_ref[...]], axis=0)
    for p, (slot, parts) in enumerate(plan):
        own = pl.multiple_of(group * share, share)
        other = pl.multiple_of((1 - group) * share, share)
        spans = {
            columns: [(start, start, wide) for start in range(0, columns, wide)],
            columns - share: [(0, own, share), (share, wide, wide), (3 * share, 2 * wide, wide)],
            share: [(0, other, share)],
        }
        for width in sorted({refs[part[0]].shape[1] for part in parts}):
            blocks = [part for part in parts if refs[part[0]].shape[1] == width]
            for start, target, size in spans[width]:
                w = jnp.concatenate(
                    [
                        refs[source][row : row + depth, start : start + size]
                        for source, row, first, depth in blocks
                    ],
                    axis=0,
                )
                both = jnp.dot(attended, w, preferred_element_type=jnp.float32)
                both = both.astype(jnp.bfloat16)
                o_buf[p, :, pl.ds(target, size)] = both[:rows]
                sent_ref[p, :, pl.ds(target, size)] = both[rows:]
        copy = pltpu.make_async_copy(
            o_buf.at[p], out_ref.at[0, :, columns_of(facts, slot, columns)], out_sem.at[p]
        )
        copy.start()
        stores.append(copy)
    for copy in stores:
        copy.wait()


def columns_of(facts, slot, columns):
    return pl.ds(pl.multiple_of(facts[ORDER + slot] * columns, columns), columns)


def place(facts, arrived, out_ref, sem):
    copies = []
    for ref, slots in arrived:
        for p, slot in enumerate(slots):
            target = out_ref.at[0, :, columns_of(facts, slot + CHIPS, ref.shape[2])]
            copy = pltpu.make_async_copy(ref.at[p], target, sem.at[len(copies)])
            copy.start()
            copies.append(copy)
    return copies


def place_kernel(slots, facts, *refs):
    before_ref, out_ref, sem = refs[-3:]
    for copy in place(facts, list(zip(refs, slots)), out_ref, sem):
        copy.wait()


def place_output(facts, arrived, before):
    blocks = [block for block, _ in arrived]
    slots = [slots for _, slots in arrived]
    return pl.pallas_call(
        partial(place_kernel, slots),
        grid_spec=pltpu.PrefetchScalarGridSpec(
            num_scalar_prefetch=1,
            grid=(),
            in_specs=[pl.BlockSpec(memory_space=pl.ANY)] * (len(blocks) + 1),
            out_specs=pl.BlockSpec(memory_space=pl.ANY),
            scratch_shapes=[pltpu.SemaphoreType.DMA((sum(map(len, slots)),))],
        ),
        out_shape=pltpu.HBM(before.shape, jnp.bfloat16),
        input_output_aliases={1 + len(blocks): 0},
        compiler_params=pltpu.CompilerParams(vmem_limit_bytes=2**20),
        name="place_output",
    )(facts, *blocks, *in_hbm([before]))


def project_output(facts, attended, before, work, arrived, width):
    rows, depth = attended[0].shape
    sources = []

    def index_of(block):
        if not any(block is held for held in sources):
            sources.append(block)
        return [block is held for held in sources].index(True)

    plan = [
        (slot, [(index_of(block), *where) for block, *where in parts]) for slot, parts in work
    ]
    held = len(sources)
    arrived = [(index_of(block), slots) for block, slots in arrived]
    placed = sum(len(slots) for _, slots in arrived)
    columns = width // (CHIPS * CORES)
    filled = [] if before is None else [before]
    return pl.pallas_call(
        partial(output_kernel, plan, arrived),
        grid_spec=pltpu.PrefetchScalarGridSpec(
            num_scalar_prefetch=1,
            grid=(),
            in_specs=[pl.BlockSpec(memory_space=pltpu.VMEM)] * (CORES + held)
            + [pl.BlockSpec(memory_space=pl.ANY)] * (len(sources) - held + len(filled)),
            out_specs=[pl.BlockSpec(memory_space=pl.ANY), pl.BlockSpec(memory_space=pltpu.VMEM)],
            scratch_shapes=[
                pltpu.VMEM((len(plan), rows, columns), jnp.bfloat16),
                pltpu.SemaphoreType.DMA((len(plan),)),
                pltpu.SemaphoreType.DMA((max(placed, 1),)),
            ],
        ),
        out_shape=[
            pltpu.HBM((1, rows, width), jnp.bfloat16),
            pltpu.VMEM((len(plan), rows, columns), jnp.bfloat16),
        ],
        input_output_aliases={1 + CORES + len(sources): 0} if filled else {},
        cost_estimate=pl.CostEstimate(flops=1000, bytes_accessed=1000, transcendentals=0),
        compiler_params=pltpu.CompilerParams(vmem_limit_bytes=(len(plan) + 8) * 2**20),
        name="project_output",
    )(facts, *attended, *sources, *in_hbm(filled))


def ring_body(
    span_states,
    recomp_states,
    w_query,
    w_kv,
    w_out,
    span_map,
    span_lengths,
    recompute_idx,
    block_table,
):
    pair = lambda ahead, back: (move(ahead, AHEAD), move(back, BACK))
    swap = lambda *blocks: tuple(move(block, SIBLING) for block in blocks)
    group = lax.axis_index("groups")
    width, heads, part = w_query.shape
    rows = recomp_states.shape[1]
    half = width // 2
    depth = heads * HD
    columns = w_out.shape[3]
    share = columns // 6
    where = (group[None].astype(jnp.int32), lax.axis_index("serve")[None].astype(jnp.int32))

    query_rows = w_query.transpose(1, 2, 0).reshape(heads * part, width)
    kv_rows = w_kv.transpose(1, 2, 0).reshape(2 * part, width)
    own_out = w_out.reshape(depth, columns)
    cut = heads * part
    k0, q0 = take_parts(
        (*where, span_lengths),
        [query_rows, kv_rows],
        [(4 * part, half), (cut, half)],
        [
            (1, 0, (0, 0), (0, 0), None, (2 * part, half)),
            (1, 0, (0, 2 * part), (half, 0), None, (2 * part, half)),
            (0, 1, (0, 0), (0, 0), False, (cut, half)),
        ],
    )
    cut = depth // 2
    theirs, top0, low0 = take_parts(
        where,
        [recomp_states[0], own_out, k0],
        [(rows, half)] + [(cut, columns - share)] * 2,
        [(0, 0, (0, 0), (0, 0), True, (rows, half))]
        + [(1, 1 + n, (n * cut, 0), (0, 0), False, (cut, share)) for n in range(2)]
        + [
            (1, 1 + n, (n * cut, 0), (2 * share, share), None, (cut, columns - 2 * share))
            for n in range(2)
        ],
    )
    facts = list_facts(*where, span_lengths, block_table)
    ka1, kb1 = together(*pair(k0, k0))
    qa1, qb1, ka1 = together(*pair(q0, q0), ka1)
    ka2, kb2, qa1 = together(*pair(ka1, kb1), qa1)
    qa2, qb2, ka2 = together(*pair(qa1, qb1), ka2)
    ka3, kb3, qa2 = together(*pair(ka2, kb2), qa2)
    qa3, qb3, ka3, top0 = together(*pair(qa2, qb2), ka3, top0)
    keys = (k0, ka1, kb1, ka2, kb2, ka3, kb3, move(kb3, BACK))
    queries = (q0, qa1, qb1, qa2, qb2, qa3, qb3, move(qa3, AHEAD))
    key_stack = (half, [(n, h * 2 * part, 2 * part) for h in range(2) for n in range(CHIPS)])
    query_stack = (half, [(CHIPS + n, 0, heads * part) for n in range(CHIPS)])
    *_, other_rows, low0, keys, queries = together(
        *keys, *queries, across(theirs), low0, packs=(key_stack, query_stack)
    )
    keys = (keys, *swap(keys))

    span0, new_kv, cache = project_kv(facts, span_states, recomp_states, keys)
    sa1, sb1 = pair(span0, span0)
    sa2, sb2 = pair(sa1, sb1)
    ta1, tb1 = together(*pair(top0, top0))
    sides = lambda *found: (share, [(n, 0, cut) for n in found])
    la1, lb1, ta1, tb1, queries, sa2, sb2, send1 = together(
        *pair(low0, low0), ta1, tb1, queries, sa2, sb2, packs=(sides(2, 0, 3, 1),)
    )
    sa3, sb3 = pair(sa2, sb2)
    mine, theirs_part = project_query(
        facts, recomp_states, other_rows, (queries, *swap(queries)), depth
    )
    ta2, tb2, la1 = together(*pair(ta1, tb1), la1)
    la2, lb2, x1, ta2, tb2, send2 = together(
        *pair(la1, lb1), across(send1), ta2, tb2, packs=(sides(3, 0, 4, 1),)
    )
    spans = (span0, sa1, sb1, sa2, sb2, sa3, sb3, move(sa3, AHEAD))
    stack = (2 * HD, [(n, 0, span0.shape[0]) for n in range(CHIPS)])
    *_, spans = together(*spans, packs=(stack,))
    other = across(theirs_part)
    attended = attend(
        span_map[0], facts, mine, other, new_kv, recompute_idx, (spans, *swap(spans))
    )
    attended = (attended, *swap(attended))
    quarter = lambda n, first: (columns - share, [(n, first, cut // 2)])
    ta3, tb3, top_ahead, top_back = together(
        *pair(ta2, tb2), packs=(quarter(0, 0), quarter(1, cut // 2))
    )
    la3, lb3, ta3, tb3, x2, send3, low_ahead, low_back = together(
        *pair(la2, lb2),
        ta3,
        tb3,
        across(send2),
        packs=(sides(2, 0, 3, 1), quarter(0, 0), quarter(1, cut // 2)),
    )

    def near(slot, top, low, side, first):
        return slot, [(top, 0, 0, cut), (low, 0, cut, cut), (side, first * depth, 0, depth)]

    early = [
        (0, [(own_out, 0, 0, depth)]),
        near(1, ta1, la1, x1, 0),
        near(2, tb1, lb1, x1, 1),
        near(3, ta2, la2, x2, 0),
        near(4, tb2, lb2, x2, 1),
    ]
    width_out = CHIPS * CORES * columns
    result, sent1 = project_output(facts, attended, None, early, [], width_out)
    t4a, t4b, l4a, l4b, x3, sent1 = lax.optimization_barrier(
        (*pair(top_ahead, top_back), *pair(low_ahead, low_back), across(send3), sent1)
    )
    x3, last_ahead, last_back = together(
        x3, packs=((share, [(0, 0, cut)]), (share, [(0, depth + cut, cut)]))
    )
    late = [near(5, ta3, la3, x3, 0), near(6, tb3, lb3, x3, 1)]
    result, sent2 = project_output(facts, attended, result, late, [], width_out)
    x4a, x4b, arrived1, sent2 = lax.optimization_barrier(
        (*pair(last_ahead, last_back), *swap(sent1), sent2)
    )
    arrived = [(arrived1, (0, 1, 2, 3, 4))]
    quarters = [(block, 0, n * cut // 2, cut // 2) for n, block in enumerate((t4a, t4b, l4a, l4b))]
    far = (7, [*quarters, (x4a, 0, 0, cut), (x4b, 0, cut, cut)])
    result, sent3 = project_output(
        facts, attended, result, [far], arrived, width_out
    )
    arrived = [(swap(sent2)[0], (5, 6)), (swap(sent3)[0], (7,))]
    return (cache, place_output(facts, arrived, result))


def solution(mesh):
    in_specs = (
        P(("groups", "serve"), None, "tensor"),
        P(("groups", "serve"), None, "tensor"),
        P("tensor", None, "serve"),
        P("tensor", None, "serve"),
        P("tensor", None, None, "serve"),
        P(("groups", "serve"), None),
        P(("groups", "serve")),
        P(("groups", "serve"), None),
        P(("groups", "serve")),
    )
    out_specs = (P(("groups", "serve"), None, None), P(("groups", "serve"), None, "tensor"))
    body = ring_body if ring_fits(mesh) else general_body
    return jax.shard_map(body, mesh=mesh, in_specs=in_specs, out_specs=out_specs, check_vma=False)
```
